32 devices in a mesh: section: 2 (over core), dp: 16 (over z, y, x).
Axes of the slice: x: 2, y: 2, z: 4, core: 2. Of those that a mesh axis runs over, the one named last changes fastest.
Arguments:
- token_ids: int32 [32, 224], P('dp'), may hold values from 0 to 50303
- seg_lengths: int32 [32, 5], P('dp'), may hold values from 1 to 112, 224 in all within a row
- rankings: int32 [32, 4], P('dp'), may hold values from 0 to 3, each once within a row
- table: float32 [1024, 50304], P('dp'), may hold values from -0.6 to 0.6
- table_m: float32 [1024, 50304], P('dp'), may hold values from -3.8146973e-06 to 3.8146973e-06
- table_v: float32 [1024, 50304], P('dp'), may hold values from 1.720838e-12 to 6.8572786e-12
- table_ema: float32 [1024, 50304], P('dp'), may hold values from -0.625 to 0.625
- in_w: float32 [2, 1024, 7168], P('section', 'dp'), may hold values from -0.1875 to 0.1875
- in_m: float32 [2, 1024, 7168], P('section', 'dp'), may hold values from -3.8146973e-06 to 3.8146973e-06
- in_v: float32 [2, 1024, 7168], P('section', 'dp'), may hold values from 1.720838e-12 to 6.8572786e-12
- in_ema: float32 [2, 1024, 7168], P('section', 'dp'), may hold values from -0.1875 to 0.1875
- out_w: float32 [2, 5120, 1024], P('section', 'dp'), may hold values from -0.75 to 0.75
- out_m: float32 [2, 5120, 1024], P('section', 'dp'), may hold values from -3.8146973e-06 to 3.8146973e-06
- out_v: float32 [2, 5120, 1024], P('section', 'dp'), may hold values from 1.720838e-12 to 6.8572786e-12
- out_ema: float32 [2, 5120, 1024], P('section', 'dp'), may hold values from -0.1875 to 0.1875
- layer_vec: float32 [2, 13312], P('section', 'dp'), may hold values from -1.2 to 2.6
- vec_m: float32 [2, 13312], P('section', 'dp'), may hold values from -1.5258789e-05 to 1.5258789e-05
- vec_v: float32 [2, 13312], P('section', 'dp'), may hold values from 2.7376967e-11 to 1.0950787e-10
- vec_ema: float32 [2, 13312], P('section', 'dp'), may hold values from -3 to 3
- final_vec: float32 [3072], P('dp'), may hold values from -1.5 to 1.5
- final_m: float32 [3072], P('dp'), may hold values from -1.9073486e-05 to 1.9073486e-05
- final_v: float32 [3072], P('dp'), may hold values from 5.21466045e-11 to 2.08586418e-10
- final_ema: float32 [3072], P('dp'), may hold values from -1.5 to 1.5
Outputs:
- loss_sum: float32 [], replicated
- grad_norm: float32 [], replicated
- table_new: float32 [1024, 50304], P('dp')
- table_m_new: float32 [1024, 50304], P('dp')
- table_v_new: float32 [1024, 50304], P('dp')
- table_ema_new: float32 [1024, 50304], P('dp')
- in_new: float32 [2, 1024, 7168], P('section', 'dp')
- in_m_new: float32 [2, 1024, 7168], P('section', 'dp')
- in_v_new: float32 [2, 1024, 7168], P('section', 'dp')
- in_ema_new: float32 [2, 1024, 7168], P('section', 'dp')
- out_new: float32 [2, 5120, 1024], P('section', 'dp')
- out_m_new: float32 [2, 5120, 1024], P('section', 'dp')
- out_v_new: float32 [2, 5120, 1024], P('section', 'dp')
- out_ema_new: float32 [2, 5120, 1024], P('section', 'dp')
- vec_new: float32 [2, 13312], P('section', 'dp')
- vec_m_new: float32 [2, 13312], P('section', 'dp')
- vec_v_new: float32 [2, 13312], P('section', 'dp')
- vec_ema_new: float32 [2, 13312], P('section', 'dp')
- final_new: float32 [3072], P('dp')
- final_m_new: float32 [3072], P('dp')
- final_v_new: float32 [3072], P('dp')
- final_ema_new: float32 [3072], P('dp')
The draws below stay inside these ranges and needn't reach their ends.
Inputs may be any that keep to these rules, and one draw needn't show every extreme that they name: `seg_lengths`: row i holds the prompt length of list i and then its 4 continuation lengths, all at least 1; each row sums to 224, and its largest entry is 112. `rankings`: each row is a permutation of 0 to 3.
All inputs are finite; a program needn't handle non-finite values.
Results may differ from the reference program's by a relative error of at most 0.029.
The reference program's roundings to bfloat16 on the way count: a program that leaves them out, or rounds other values in their place, can miss the bound.
Values may be sent and summed in bfloat16 or wider, within the bound.
No kernel may reach another device: no remote copies, remote signals or barrier semaphores. Data moves between devices by JAX's collectives and lax.ppermute only.
A program may use at most 448 MiB of HBM per device.

```python
import math
import jax
import jax.numpy as jnp
import numpy as np
from jax import lax

D = 1024
HEADS = 16
HEAD_DIM = 64
FF = 4096
V = 50304
ROT = 16
K = 4
L = 224
STEP = 10
LAYERS = 2
LISTS = 32
NPARAMS = 76706816


def draw_out_w(key, part):
    key = jax.random.fold_in(key, 11)
    noise = jnp.clip(jax.random.normal(key, (LAYERS, D + FF, D), jnp.float32), -6.0, 6.0)
    row_index = jnp.arange(D + FF)[None, :, None]
    scale_factor = jnp.where(row_index < D, 4.0 * D ** (-0.5), FF ** (-0.5))
    return noise * scale_factor


def draw_layer_vec(key, part):
    key = jax.random.fold_in(key, 12)
    key_gain, key_bias = jax.random.split(key)
    column = jnp.arange(9 * D + FF)
    within = (column % D).astype(jnp.float32) / D
    is_gain = (column < 4 * D) & (column // D % 2 == 0)
    gains = (0.5 + 1.5 * within) * jax.random.uniform(key_gain, (LAYERS, 9 * D + FF), jnp.float32, 0.7, 1.3)
    biases = 0.2 * jnp.clip(jax.random.normal(key_bias, (LAYERS, 9 * D + FF), jnp.float32), -6.0, 6.0)
    return jnp.where(is_gain[None, :], gains, biases)


def draw_final_vec(key, part):
    key = jax.random.fold_in(key, 13)
    key_gain, key_rest = jax.random.split(key)
    column = jnp.arange(3 * D)
    within = (column % D).astype(jnp.float32) / D
    gains = (0.125 + 0.375 * within) * jax.random.uniform(key_gain, (3 * D,), jnp.float32, 0.7, 1.3)
    noise = jnp.clip(jax.random.normal(key_rest, (3 * D,), jnp.float32), -6.0, 6.0)
    rest = jnp.where(column < 2 * D, 0.05 * noise, 8.0 * D ** (-0.5) * noise)
    return jnp.where(column < D, gains, rest)


def draw_final_v(key, part):
    key = jax.random.fold_in(key, 14)
    lowest = 0.004 / NPARAMS
    uniform_part = jax.random.uniform(key, (3 * D,), jnp.float32, 0.0, 1.0)
    return lowest * jnp.exp(uniform_part * 1.3862943611198906)


def place_ends(drawn, stream_key, low, largest):
    spot = [jax.random.randint(jax.random.fold_in(stream_key, axis), (), 0, length) for axis, length in enumerate(drawn.shape)]
    longest = drawn.shape.index(max(drawn.shape))
    next_to = spot[:longest] + [(spot[longest] + 1) % drawn.shape[longest]] + spot[longest + 1:]
    return drawn.at[tuple(spot)].set(low).at[tuple(next_to)].set(largest)


def levels(key, shape, shards, smallest, high):
    loudness, own = 1.0, jax.random.fold_in(key, 6)
    for axis_at, blocks in shards:
        steps = jnp.exp(jax.random.uniform(jax.random.fold_in(own, axis_at), (blocks,), jnp.float32, smallest / len(shards), high / len(shards)))
        loudness = loudness * jnp.repeat(steps, shape[axis_at] // blocks).reshape([-1 if axis == axis_at else 1 for axis in range(len(shape))])
    return loudness


def cumulative_ranks(count, lean):
    loads = [(1 << 20) // math.isqrt(rank ** lean) + 1 for rank in range(1, count + 1)]
    scale = 1 + sum(loads) // (1 << 30)
    return np.cumsum(np.array([max(1, weight // scale) for weight in loads]))


def ranked(rng, dims, count, skew):
    table = cumulative_ranks(count, skew)
    ticket = jax.random.randint(jax.random.fold_in(rng, 1), dims, 0, int(table[count - 1]))
    rank = jnp.searchsorted(jnp.asarray(table, jnp.int32), ticket, side="right")
    return jax.random.permutation(jax.random.fold_in(rng, 2), count)[rank].astype(jnp.int32)


def profile(number_of, total, limit, slope):
    weights = [(1 << 20) // math.isqrt(standing ** slope) + 1 for standing in range(2, number_of + 1)]
    spare, given = total - limit - (number_of - 1), [1] * (number_of - 1)
    while spare > 0:
        movable = [i for i in range(number_of - 1) if given[i] < limit]
        pool, left = sum([weights[i] for i in movable]), spare
        for i in movable:
            addition = min(limit - given[i], max(1, left * weights[i] // pool), spare)
            given[i] = given[i] + addition
            spare = spare - addition
    return np.array([limit] + given)


def uneven(rng, count, total, bound, skew):
    if count == 2:
        one = jax.random.randint(rng, (), max(1, total - bound), min(bound, total - 1) + 1)
        return jnp.stack([one, total - one])
    sizes = jnp.asarray(profile(count, total, bound, skew), jnp.int32)
    couples = (count - 1) // 2
    donor, taker = sizes[1:1 + 2 * couples:2], sizes[2:2 + 2 * couples:2]
    slack = jnp.minimum(donor - 1, bound - taker)
    moved = jax.random.randint(jax.random.fold_in(rng, 1), (couples,), 0, 1 << 20) % (slack + 1)
    sizes = sizes.at[1:1 + 2 * couples:2].set(donor - moved).at[2:2 + 2 * couples:2].set(taker + moved)
    return sizes[jax.random.permutation(jax.random.fold_in(rng, 2), count)]


def gaussian(key, dims, deviation, most, cuts=(), kind=jnp.bfloat16):
    array = jax.random.normal(key, dims, jnp.float32) * deviation
    if len(cuts) > 0:
        array = levels(key, dims, cuts, -0.22, 0.18) * array
    return jnp.clip(array, min=-most, max=most).astype(kind)


def setup_inputs(seed: int = 0) -> dict:
    streams_of = jax.random.split(jax.random.key(seed), 24)
    token_ids = place_ends(ranked(streams_of[0], (LISTS, L), V, 2), jax.random.fold_in(streams_of[0], 3), 0, V - 1).astype(jnp.int32)
    seg_lengths = jax.vmap(lambda own: uneven(own, K + 1, L, L // 2, 2))(jax.random.split(streams_of[1], LISTS)).reshape((LISTS, K + 1)).astype(jnp.int32)
    rankings = jax.vmap(lambda own: jax.random.permutation(own, K))(jax.random.split(streams_of[2], LISTS)).reshape((LISTS, K)).astype(jnp.int32)
    table = gaussian(streams_of[3], (D, V), 0.1, 0.6, ((0, 16),), jnp.float32)
    table_m = gaussian(streams_of[4], (D, V), (0.0055 * NPARAMS ** -0.5), 3.814697265625e-06, ((0, 16),), jnp.float32)
    table_v = jnp.clip(jnp.exp(math.log(6.8572786338094716e-12) - 1.3824993 * jax.random.uniform(streams_of[5], (D, V), jnp.float32) ** levels(streams_of[5], (D, V), ((0, 16),), -0.2, 0.2)), 1.720837990333568e-12, 6.8572786338094716e-12)
    table_ema = gaussian(streams_of[6], (D, V), 0.1, 0.625, ((0, 16),), jnp.float32)
    in_w = gaussian(streams_of[7], (LAYERS, D, 3 * D + FF), D ** -0.5, 0.1875, ((0, 2), (1, 16)), jnp.float32)
    in_m = gaussian(streams_of[8], (LAYERS, D, 3 * D + FF), (0.0055 * NPARAMS ** -0.5), 3.814697265625e-06, ((0, 2), (1, 16)), jnp.float32)
    in_v = jnp.clip(jnp.exp(math.log(6.8572786338094716e-12) - 1.3824993 * jax.random.uniform(streams_of[9], (LAYERS, D, 3 * D + FF), jnp.float32) ** levels(streams_of[9], (LAYERS, D, 3 * D + FF), ((0, 2), (1, 16)), -0.2, 0.2)), 1.720837990333568e-12, 6.8572786338094716e-12)
    in_ema = gaussian(streams_of[10], (LAYERS, D, 3 * D + FF), D ** -0.5, 0.1875, ((0, 2), (1, 16)), jnp.float32)
    out_w = draw_out_w(jax.random.fold_in(streams_of[23], 71), 0)
    out_m = gaussian(streams_of[12], (LAYERS, D + FF, D), (0.0055 * NPARAMS ** -0.5), 3.814697265625e-06, ((0, 2), (1, 16)), jnp.float32)
    out_v = jnp.clip(jnp.exp(math.log(6.8572786338094716e-12) - 1.3824993 * jax.random.uniform(streams_of[13], (LAYERS, D + FF, D), jnp.float32) ** levels(streams_of[13], (LAYERS, D + FF, D), ((0, 2), (1, 16)), -0.2, 0.2)), 1.720837990333568e-12, 6.8572786338094716e-12)
    out_ema = gaussian(streams_of[14], (LAYERS, D + FF, D), D ** -0.5, 0.1875, ((0, 2), (1, 16)), jnp.float32)
    layer_vec = draw_layer_vec(jax.random.fold_in(streams_of[23], 71), 0)
    vec_m = gaussian(streams_of[16], (LAYERS, 9 * D + FF), (0.022 * NPARAMS ** -0.5), 1.52587890625e-05, ((0, 2), (1, 16)), jnp.float32)
    vec_v = jnp.clip(jnp.exp(math.log(1.0950786805130619e-10) - 1.3862944 * jax.random.uniform(streams_of[17], (LAYERS, 9 * D + FF), jnp.float32) ** levels(streams_of[17], (LAYERS, 9 * D + FF), ((0, 2), (1, 16)), -0.2, 0.2)), 2.7376967012826547e-11, 1.0950786805130619e-10)
    vec_ema = gaussian(streams_of[18], (LAYERS, 9 * D + FF), 0.5, 3.0, ((0, 2), (1, 16)), jnp.float32)
    final_vec = draw_final_vec(jax.random.fold_in(streams_of[23], 71), 0)
    final_m = gaussian(streams_of[20], (3 * D,), (0.03 * NPARAMS ** -0.5), 1.9073486328125e-05, ((0, 16),), jnp.float32)
    final_v = draw_final_v(jax.random.fold_in(streams_of[23], 71), 0)
    final_ema = gaussian(streams_of[22], (3 * D,), 0.25, 1.5, ((0, 16),), jnp.float32)
    return {"token_ids": token_ids, "seg_lengths": seg_lengths, "rankings": rankings, "table": table, "table_m": table_m, "table_v": table_v, "table_ema": table_ema, "in_w": in_w, "in_m": in_m, "in_v": in_v, "in_ema": in_ema, "out_w": out_w, "out_m": out_m, "out_v": out_v, "out_ema": out_ema, "layer_vec": layer_vec, "vec_m": vec_m, "vec_v": vec_v, "vec_ema": vec_ema, "final_vec": final_vec, "final_m": final_m, "final_v": final_v, "final_ema": final_ema}


@jax.custom_vjp
def low(v):
    return lax.optimization_barrier(v.astype(jnp.bfloat16)).astype(jnp.float32)

@jax.custom_vjp
def low_back(v):
    return v

def low_keep(v):
    return (low(v), None)

def low_pass(kept, grad):
    return (grad,)

def back_keep(v):
    return (v, None)

def back_low(kept, grad):
    return (low(grad),)
low.defvjp(low_keep, low_pass)
low_back.defvjp(back_keep, back_low)
EPS_NORM = 1e-05
CLIP_NORM = 0.05
BETA_ONE = 0.9
BETA_TWO = 0.95
ADAM_EPS = 1e-08
RATE_MAT = 0.1
RATE_VEC = 0.3
WEIGHT_DECAY = 0.1
EMA_KEEP = 0.75
MASKED = -1e+30
PRECISE = lax.Precision.HIGHEST

def product(left_operand, right_operand):
    return jnp.dot(left_operand, right_operand, precision=PRECISE, preferred_element_type=jnp.float32)

def norm_rows(value_rows, gain_vector, bias_vector):
    center = value_rows - lax.optimization_barrier(jnp.mean(value_rows, -1, keepdims=True))
    spread = lax.optimization_barrier(jnp.mean(center * center, -1, keepdims=True))
    return center * lax.rsqrt(spread + EPS_NORM) * gain_vector + bias_vector

def layout(lengths, width):
    bounds = jnp.cumsum(lengths).astype(jnp.int32)
    starts = bounds - lengths
    places = jnp.arange(width, dtype=jnp.int32)
    segment = lax.optimization_barrier(jnp.sum((places[:, None] >= bounds[None, :]).astype(jnp.int32), 1))
    pieces_count = lengths.shape[0]
    owner = jnp.minimum(segment, pieces_count - 1)
    chosen = jnp.arange(pieces_count, dtype=jnp.int32)[None, :] == owner[:, None]
    begin = lax.optimization_barrier(jnp.sum(jnp.where(chosen, starts[None, :], 0), 1))
    position = places - begin + jnp.where(segment > 0, lengths[0], 0)
    same = (segment[:, None] == segment[None, :]) & (places[None, :] <= places[:, None])
    prompt = (segment[None, :] == 0) & (segment[:, None] > 0) & (segment[:, None] < pieces_count)
    return (position, same | prompt, bounds[1:] - 1)

def angles(position):
    half = ROT // 2
    freqs = 10000.0 ** (-2.0 * jnp.arange(half, dtype=jnp.float32) / ROT)
    phase = position.astype(jnp.float32)[:, None] * freqs[None, :]
    return (jnp.cos(phase)[:, None, :], jnp.sin(phase)[:, None, :])

def turn(value_rows, cosine, sine, sign):
    half = cosine.shape[-1]
    first = value_rows[..., :half]
    second = value_rows[..., half:2 * half]
    return jnp.concatenate([first * cosine - sign * second * sine, second * cosine + sign * first * sine, value_rows[..., 2 * half:]], -1)

def pieces(vector):
    amounts = [D, D, D, D, 3 * D, D, FF, D]
    parts = []
    offset = 0
    for amount in amounts:
        parts.append(vector[offset:offset + amount])
        offset = offset + amount
    return parts

def block_layer(residual_state, w_in, w_out, vector, cosine, sine, allowed):
    rows = residual_state.shape[0]
    first_gain, first_bias, second_gain, second_bias, bias_qkv, bias_attn, bias_up, bias_down = pieces(vector)
    left_operand = low(norm_rows(residual_state, first_gain, first_bias))
    right_operand = low(norm_rows(residual_state, second_gain, second_bias))
    joined = low_back(product(left_operand, w_in[:, :3 * D]) + bias_qkv)
    upper_projection = low_back(product(right_operand, w_in[:, 3 * D:]) + bias_up)
    query_rows = low(turn(joined[:, :D].reshape(rows, HEADS, HEAD_DIM), cosine, sine, 1.0))
    key_rows = low(turn(joined[:, D:2 * D].reshape(rows, HEADS, HEAD_DIM), cosine, sine, 1.0))
    value_rows = low(joined[:, 2 * D:].reshape(rows, HEADS, HEAD_DIM))
    scores = low_back(jnp.einsum('qhe,khe->hqk', query_rows, key_rows, precision=PRECISE) * HEAD_DIM ** (-0.5))
    weights = low(jax.nn.softmax(jnp.where(allowed[None], scores, MASKED), -1))
    mixed_output = low(low_back(jnp.einsum('hqk,khe->qhe', weights, value_rows, precision=PRECISE).reshape(rows, D)))
    active_flags = low(jax.nn.gelu(upper_projection, approximate=False))
    branch = product(mixed_output, w_out[:D]) + bias_attn + (product(active_flags, w_out[D:]) + bias_down)
    return residual_state + low_back(branch)

def plackett(scores, ranking):
    ordered = scores[ranking]
    count = ordered.shape[0]
    later = jnp.arange(count)[None, :] >= jnp.arange(count)[:, None]
    grid = jnp.where(later, ordered[None, :], MASKED)
    top_score = lax.optimization_barrier(jnp.max(grid, 1, keepdims=True))
    tails = top_score[:, 0] + jnp.log(lax.optimization_barrier(jnp.sum(jnp.exp(grid - top_score), 1)))
    return jnp.sum(tails - ordered)

def list_loss(params, tokens, lengths, ranking):
    table, w_in, w_out, vectors, final = params
    position, allowed, final_position = layout(lengths, L)
    cosine, sine = angles(position)
    residual_state = low_back(table[:, tokens].T)
    for layer_index in range(LAYERS):
        if layer_index > 0:
            residual_state = low_back(low(residual_state))
        residual_state = block_layer(residual_state, w_in[layer_index], w_out[layer_index], vectors[layer_index], cosine, sine, allowed)
    selected_entries = low(norm_rows(residual_state[final_position], final[:D], final[D:2 * D]))
    return plackett(lax.optimization_barrier(jnp.sum(selected_entries * final[2 * D:], -1)), ranking)

def group_loss(params, tokens, lengths, ranking):
    rounded = tuple((low(weight) for weight in params))

    def single(total_value, item):
        return (total_value + list_loss(rounded, item[0], item[1], item[2]), None)
    total_value, _ = lax.scan(jax.checkpoint(single), jnp.zeros((), params[0].dtype), (tokens, lengths, ranking))
    return total_value

def adamw_update(weight, moment, second, average, gradient_value, rate, decay):
    moment_new = BETA_ONE * moment + (1.0 - BETA_ONE) * gradient_value
    second_new = BETA_TWO * second + (1.0 - BETA_TWO) * gradient_value * gradient_value
    moment_hat = moment_new / (1.0 - BETA_ONE ** STEP)
    second_hat = second_new / (1.0 - BETA_TWO ** STEP)
    weight_new = weight - rate * (moment_hat / (jnp.sqrt(second_hat) + ADAM_EPS) + decay * weight)
    average_new = EMA_KEEP * average + (1.0 - EMA_KEEP) * weight_new
    return (weight_new, moment_new, second_new, average_new)

def reference(token_ids, seg_lengths, rankings, table, table_m, table_v, table_ema, in_w, in_m, in_v, in_ema, out_w, out_m, out_v, out_ema, layer_vec, vec_m, vec_v, vec_ema, final_vec, final_m, final_v, final_ema):
    params = (table, in_w, out_w, layer_vec, final_vec)
    groups = LISTS // 8
    data = (token_ids.reshape(groups, 8, L), seg_lengths.reshape(groups, 8, K + 1), rankings.reshape(groups, 8, K))

    def accumulate(carry, item):
        total_value, grads = carry
        value, pull = jax.vjp(lambda weights: group_loss(weights, item[0], item[1], item[2]), params)
        fresh, = pull(jnp.ones((), value.dtype))
        return ((total_value + value, jax.tree.map(jnp.add, grads, fresh)), None)
    zeros = jax.tree.map(jnp.zeros_like, params)
    (loss_sum, grads), _ = lax.scan(accumulate, (jnp.zeros((), table.dtype), zeros), data)
    squares = sum((jnp.sum(gradient_value * gradient_value) for gradient_value in grads))
    grad_norm = jnp.sqrt(squares)
    factor = jnp.minimum(1.0, CLIP_NORM / (grad_norm + 1e-06))
    table_new, table_m_new, table_v_new, table_ema_new = adamw_update(table, table_m, table_v, table_ema, grads[0] * factor, RATE_MAT, WEIGHT_DECAY)
    in_new, in_m_new, in_v_new, in_ema_new = adamw_update(in_w, in_m, in_v, in_ema, grads[1] * factor, RATE_MAT, WEIGHT_DECAY)
    out_new, out_m_new, out_v_new, out_ema_new = adamw_update(out_w, out_m, out_v, out_ema, grads[2] * factor, RATE_MAT, WEIGHT_DECAY)
    vec_new, vec_m_new, vec_v_new, vec_ema_new = adamw_update(layer_vec, vec_m, vec_v, vec_ema, grads[3] * factor, RATE_VEC, 0.0)
    final_new, final_m_new, final_v_new, final_ema_new = adamw_update(final_vec, final_m, final_v, final_ema, grads[4] * factor, RATE_VEC, 0.0)
    return (loss_sum, grad_norm, table_new, table_m_new, table_v_new, table_ema_new, in_new, in_m_new, in_v_new, in_ema_new, out_new, out_m_new, out_v_new, out_ema_new, vec_new, vec_m_new, vec_v_new, vec_ema_new, final_new, final_m_new, final_v_new, final_ema_new)
```

```python
import jax
import jax.numpy as jnp
from jax import lax
from jax.sharding import PartitionSpec as P

D = 1024
HEADS = 16
HEAD_DIM = 64
FF = 4096
ROT = 16
STEP = 10


EPS_NORM = 1e-05
CLIP_NORM = 0.05
BETA_ONE = 0.9
BETA_TWO = 0.95
ADAM_EPS = 1e-08
RATE_MAT = 0.1
RATE_VEC = 0.3
WEIGHT_DECAY = 0.1
EMA_KEEP = 0.75
MASKED = -1e30


def matmul(left_operand, right_operand):
    return jnp.dot(left_operand, right_operand, preferred_element_type=jnp.float32)


def dot_rows(left_operand, right_operand):
    return lax.dot_general(
        left_operand, right_operand, (((0,), (0,)), ((), ())), preferred_element_type=jnp.float32
    )


def dot_cols(left_operand, right_operand):
    return lax.dot_general(
        left_operand, right_operand, (((1,), (1,)), ((), ())), preferred_element_type=jnp.float32
    )


def standard_deviation(value_rows):
    center = value_rows - jnp.mean(value_rows, -1, keepdims=True)
    scale_factor = lax.rsqrt(jnp.mean(center * center, -1, keepdims=True) + EPS_NORM)
    return (center * scale_factor, scale_factor)


def norm_gradient_pass(gradient_normalized, input_normalized, scale_factor):
    return scale_factor * (
        gradient_normalized
        - jnp.mean(gradient_normalized, -1, keepdims=True)
        - input_normalized * jnp.mean(gradient_normalized * input_normalized, -1, keepdims=True)
    )


def layout(lengths, width):
    bounds = jnp.cumsum(lengths)
    starts = bounds - lengths
    places = jnp.arange(width, dtype=jnp.int32)
    segment = jnp.sum((places[:, None] >= bounds[None, :]).astype(jnp.int32), 1)
    pieces_count = lengths.shape[0]
    owner = jnp.minimum(segment, pieces_count - 1)
    chosen = jnp.arange(pieces_count, dtype=jnp.int32)[None, :] == owner[:, None]
    begin = jnp.sum(jnp.where(chosen, starts[None, :], 0), 1)
    position = places - begin + jnp.where(segment > 0, lengths[0], 0)
    same = (segment[:, None] == segment[None, :]) & (places[None, :] <= places[:, None])
    prompt = (segment[None, :] == 0) & (segment[:, None] > 0) & (segment[:, None] < pieces_count)
    return (position, same | prompt, bounds[1:] - 1)


def angles(position):
    half = ROT // 2
    freqs = 10000.0 ** (-2.0 * jnp.arange(half, dtype=jnp.float32) / ROT)
    phase = position.astype(jnp.float32)[:, None] * freqs[None, :]
    return (jnp.cos(phase)[:, None, :], jnp.sin(phase)[:, None, :])


def turn(value_rows, cosine, sine, sign):
    half = cosine.shape[-1]
    first = value_rows[..., :half]
    second = value_rows[..., half : 2 * half]
    return jnp.concatenate(
        [
            first * cosine - sign * second * sine,
            second * cosine + sign * first * sine,
            value_rows[..., 2 * half :],
        ],
        -1,
    )


def pieces(vector):
    amounts = [D, D, D, D, 3 * D, D, FF, D]
    parts = []
    offset = 0
    for amount in amounts:
        parts.append(vector[offset : offset + amount])
        offset = offset + amount
    return parts


def gelu_slope(value_rows):
    cumulative = 0.5 * (1.0 + jax.scipy.special.erf(value_rows * 0.7071067811865476))
    return cumulative + value_rows * jnp.exp(-0.5 * value_rows * value_rows) * 0.3989422804014327


def scores_of(query_rows, key_rows, allowed):
    raw = jnp.einsum(
        "qhe,khe->hqk", query_rows, key_rows, preferred_element_type=jnp.float32
    ) * HEAD_DIM ** (-0.5)
    return jnp.where(allowed[None], raw, MASKED)


def grid(count):
    return {16: (4, 2, 2), 128: (8, 4, 4)}.get(count, (count, 1, 1))


class Links:
    def __init__(self):
        self.count = lax.axis_size("dp")
        self.sizes = grid(self.count)
        self.nz, self.n1, self.n2 = self.sizes
        self.core = lax.axis_index("section")
        self.dp = lax.axis_index("dp")
        self.z = self.dp // (self.n1 * self.n2)
        self.i1 = self.dp // self.n2 % self.n1
        self.i2 = self.dp % self.n2
        self.twist = self.n1 == self.n2
        self.na, self.nb = self.n2, self.n1

    def axis_of(self, kind, core):
        if kind == "z":
            return 0
        if kind == "a":
            return 1 if core == 1 and self.twist else 2
        if kind == "b":
            return 2 if core == 1 and self.twist else 1
        return kind

    def pairs(self, kind, target):
        result = []
        for core in range(2):
            axis = self.axis_of(kind, core)
            for place in range(self.count):
                spot = [place // (self.n1 * self.n2), place // self.n2 % self.n1, place % self.n2]
                spot[axis] = target(spot[axis], self.sizes[axis])
                to = (spot[0] * self.n1 + spot[1]) * self.n2 + spot[2]
                result.append((core * self.count + place, core * self.count + to))
        return result

    def shift(self, value, kind, steps=1):
        pairs = self.pairs(kind, lambda place, size: (place + steps) % size)
        return lax.ppermute(value, ("section", "dp"), pairs)

    def flip(self, value, kind, bit):
        return lax.ppermute(value, ("section", "dp"), self.pairs(kind, lambda place, size: place ^ bit))

    def swap(self, value):
        return lax.ppermute(value, "section", [(0, 1), (1, 0)])

    def plane(self, back_a, back_b, core):
        first = (self.i1 - back_b) % self.n1
        second = (self.i2 - back_a) % self.n2
        usual = first * self.n2 + second
        if not self.twist:
            return usual
        other = (self.i1 - back_a) % self.n1 * self.n2 + (self.i2 - back_b) % self.n2
        return jnp.where(core == 0, usual, other)


def update(whole, part, starts):
    starts = [jnp.asarray(start, jnp.int32) for start in starts]
    starts = starts + [jnp.zeros((), jnp.int32)] * (whole.ndim - len(starts))
    return lax.dynamic_update_slice(whole, part, starts)


def collect_layers_first(links, shard):
    rows, width = shard.shape
    nz, na, nb = links.nz, links.na, links.nb
    column = jnp.zeros((nz, rows, width), shard.dtype)
    piece = shard
    for step in range(nz):
        if step > 0:
            piece = links.shift(piece, "z")
        column = update(column, piece[None], [(links.z - step) % nz])
    whole = jnp.zeros((nz, na * nb, 2, rows, width), shard.dtype)
    along = column
    for back_a in range(na):
        if back_a > 0:
            along = links.shift(along, "a")
        across = along
        for back_b in range(nb):
            if back_b > 0:
                across = links.shift(across, "b")
            sibling = links.swap(across)
            mine = links.plane(back_a, back_b, links.core)
            theirs = links.plane(back_a, back_b, 1 - links.core)
            whole = update(whole, across[:, None, None], [0, mine, links.core])
            whole = update(whole, sibling[:, None, None], [0, theirs, 1 - links.core])
    return whole.reshape(nz * na * nb * 2 * rows, width)


def collect_layers_last(links, shard):
    rows, width = shard.shape
    nz, na, nb = links.nz, links.na, links.nb
    layer = jnp.zeros((na * nb, rows, width), shard.dtype)
    along = shard
    for back_a in range(na):
        if back_a > 0:
            along = links.shift(along, "a")
        across = along
        for back_b in range(nb):
            if back_b > 0:
                across = links.shift(across, "b")
            layer = update(layer, across[None], [links.plane(back_a, back_b, links.core)])
    whole = jnp.zeros((nz, na * nb, 2, rows, width), shard.dtype)
    for step in range(nz):
        if step > 0:
            layer = links.shift(layer, "z")
        sibling = links.swap(layer)
        place = (links.z - step) % nz
        whole = update(whole, layer[None, :, None], [place, 0, links.core])
        whole = update(whole, sibling[None, :, None], [place, 0, 1 - links.core])
    return whole.reshape(nz * na * nb * 2 * rows, width)


def collect_small(links, row):
    pieces = [row]
    for _ in range(links.nz - 1):
        pieces.append(links.shift(pieces[-1], "z"))
    stack = jnp.stack(pieces)
    parts, places = [], []
    along = stack
    for back_a in range(links.na):
        if back_a > 0:
            along = links.shift(along, "a")
        across = along
        for back_b in range(links.nb):
            if back_b > 0:
                across = links.shift(across, "b")
            parts.append(across)
            plane = links.plane(back_a, back_b, links.core)
            for step in range(links.nz):
                places.append((links.z - step) % links.nz * (links.n1 * links.n2) + plane)
    found = jnp.concatenate(parts)
    return place_rows(found, jnp.stack(places))


def place_rows(found, places):
    count = found.shape[0]
    result = jnp.zeros_like(found)
    spots = jnp.arange(count, dtype=jnp.int32)
    for index in range(count):
        chosen = spots == places[index]
        result = jnp.where(chosen[(slice(None),) + (None,) * (found.ndim - 1)], found[index][None], result)
    return result


def roll_to(value, axis, first):
    size = value.shape[axis]
    if size == 1:
        return value
    doubled = jnp.concatenate([value, value], axis)
    return lax.dynamic_slice_in_dim(doubled, first, size, axis)


def relative_rows(links, left):
    features = left.shape[1]
    nz, n1, n2 = links.sizes
    half = features // (links.count * 2)
    turned = left.T.reshape(nz, n1, n2, 2, half, left.shape[0])
    turned = roll_to(roll_to(roll_to(turned, 0, links.z), 1, links.i1), 2, links.i2)
    turned = roll_to(turned, 3, links.core)
    ordinary = turned.transpose(3, 2, 1, 0, 4, 5)
    if not links.twist:
        return ordinary
    other = turned.transpose(3, 1, 2, 0, 4, 5)
    return jnp.stack(
        [jnp.where(links.core == 0, ordinary[0], other[0]), jnp.where(links.core == 0, other[1], ordinary[1])]
    )


def reduce_layers_first(links, left, right):
    nz, na, nb = links.nz, links.na, links.nb
    half, width = left.shape[4], right.shape[1]
    rows = left.shape[5]
    give = matmul(left[1].reshape(-1, rows), right).astype(jnp.bfloat16)
    got = links.swap(give)
    total = matmul(left[0].reshape(-1, rows), right) + got.astype(jnp.float32)
    total = total.astype(jnp.bfloat16).reshape(na, nb, nz, half, width)
    lines = []
    for at_a in range(na):
        moving = total[at_a, nb - 1]
        for at_b in range(nb - 2, -1, -1):
            moving = add_low(total[at_a, at_b], links.shift(moving, "b"))
        lines.append(moving)
    moving = lines[na - 1]
    for at_a in range(na - 2, -1, -1):
        moving = add_low(lines[at_a], links.shift(moving, "a"))
    column = moving
    moving = column[nz - 1]
    for at_z in range(nz - 2, -1, -1):
        moved = links.shift(moving, "z")
        moving = column[at_z].astype(jnp.float32) + moved.astype(jnp.float32)
        if at_z > 0:
            moving = moving.astype(jnp.bfloat16)
    return moving.astype(jnp.float32)


def reduce_layers_last(links, left, right):
    nz, na, nb = links.nz, links.na, links.nb
    half, width = left.shape[4], right.shape[1]
    rows = left.shape[5]
    left = left.transpose(0, 3, 1, 2, 4, 5)
    give = matmul(left[1].reshape(-1, rows), right).astype(jnp.bfloat16)
    got = links.swap(give)
    total = matmul(left[0].reshape(-1, rows), right) + got.astype(jnp.float32)
    total = total.astype(jnp.bfloat16).reshape(nz, na, nb, half, width)
    moving = total[nz - 1]
    for at_z in range(nz - 2, -1, -1):
        moving = add_low(total[at_z], links.shift(moving, "z"))
    layer = moving
    lines = []
    for at_a in range(na):
        moving = layer[at_a, nb - 1]
        for at_b in range(nb - 2, -1, -1):
            moving = add_low(layer[at_a, at_b], links.shift(moving, "b"))
        lines.append(moving)
    moving = lines[na - 1]
    for at_a in range(na - 2, -1, -1):
        moved = links.shift(moving, "a")
        moving = lines[at_a].astype(jnp.float32) + moved.astype(jnp.float32)
        if at_a > 0:
            moving = moving.astype(jnp.bfloat16)
    return moving.astype(jnp.float32)


def add_low(first, second):
    return (first.astype(jnp.float32) + second.astype(jnp.float32)).astype(jnp.bfloat16)


def exchange(links, blocks):
    nz, n1, n2 = links.sizes
    blocks = blocks.reshape((nz, n1, n2) + blocks.shape[1:])
    for axis, here in ((2, links.i2), (1, links.i1), (0, links.z)):
        size = links.sizes[axis]
        fresh = blocks
        for steps in range(1, size):
            part = lax.dynamic_slice_in_dim(blocks, (here + steps) % size, 1, axis)
            moved = links.shift(part, axis, steps)
            fresh = lax.dynamic_update_slice_in_dim(fresh, moved, (here - steps) % size, axis)
        blocks = fresh
    return blocks.reshape((nz * n1 * n2,) + blocks.shape[3:])


def all_sum(links, value):
    value = value + links.swap(value)
    for axis in (2, 1, 0):
        bit = 1
        while bit < links.sizes[axis]:
            value = value + links.flip(value, axis, bit)
            bit = bit * 2
    return value


def softmax_parts(scores):
    top_score = jnp.max(scores, -1, keepdims=True)
    powers = jnp.exp(scores - top_score)
    return powers / jnp.sum(powers, -1, keepdims=True)


def first_layer_forward(state, w_qkv, w_up, w_out, vector, cosine, sine, allowed):
    rows = state.shape[0]
    first_gain, first_bias, second_gain, second_bias, bias_qkv, bias_attn, bias_up, bias_down = pieces(vector)
    normal, scale = standard_deviation(state)
    left = (normal * first_gain + first_bias).astype(jnp.bfloat16)
    right = (normal * second_gain + second_bias).astype(jnp.bfloat16)
    joined = matmul(left, w_qkv) + bias_qkv
    upper = matmul(right, w_up) + bias_up
    query = turn(joined[:, :D].reshape(rows, HEADS, HEAD_DIM), cosine, sine, 1.0).astype(jnp.bfloat16)
    keys = turn(joined[:, D : 2 * D].reshape(rows, HEADS, HEAD_DIM), cosine, sine, 1.0).astype(jnp.bfloat16)
    values = joined[:, 2 * D :].reshape(rows, HEADS, HEAD_DIM).astype(jnp.bfloat16)
    weights = softmax_parts(scores_of(query, keys, allowed))
    mixed = (
        jnp.einsum("hqk,khe->qhe", weights.astype(jnp.bfloat16), values, preferred_element_type=jnp.float32)
        .reshape(rows, D)
        .astype(jnp.bfloat16)
    )
    active = jax.nn.gelu(upper, approximate=False).astype(jnp.bfloat16)
    acts = jnp.concatenate([mixed, active], 1)
    branch = matmul(mixed, w_out[:D]) + bias_attn + (matmul(active, w_out[D:]) + bias_down)
    kept = (normal, scale, left, right, upper, query, keys, values, weights, acts)
    return (state + branch, kept)


def attention_backward(query, keys, values, weights, grad_mixed):
    factor = HEAD_DIM ** (-0.5)
    grad_weights = jnp.einsum("qhe,khe->hqk", grad_mixed, values, preferred_element_type=jnp.float32)
    grad_scores = (weights * (grad_weights - jnp.sum(weights * grad_weights, -1, keepdims=True))).astype(jnp.bfloat16)
    grad_values = jnp.einsum(
        "hqk,qhe->khe", weights.astype(jnp.bfloat16), grad_mixed, preferred_element_type=jnp.float32
    )
    grad_query = jnp.einsum("hqk,khe->qhe", grad_scores, keys, preferred_element_type=jnp.float32) * factor
    grad_keys = jnp.einsum("hqk,qhe->khe", grad_scores, query, preferred_element_type=jnp.float32) * factor
    return (grad_query, grad_keys, grad_values)


def total_rows(value):
    return jnp.sum(value.astype(jnp.float32), 0)


def plackett(scores, ranking):
    ordered = scores[ranking]
    count = ordered.shape[0]
    later = jnp.arange(count)[None, :] >= jnp.arange(count)[:, None]
    grid = jnp.where(later, ordered[None, :], MASKED)
    top_score = jnp.max(grid, 1, keepdims=True)
    tails = top_score[:, 0] + jnp.log(jnp.sum(jnp.exp(grid - top_score), 1))
    return jnp.sum(tails - ordered)


def head_pass(state, final, ranking):
    gain_vector, bias_vector, weight = (final[:D], final[D : 2 * D], final[2 * D :])
    normal, scale = standard_deviation(state)
    chosen = lax.reduce_precision(normal * gain_vector + bias_vector, 8, 7)
    scores = jnp.sum(chosen * weight, -1)
    loss, pull = jax.vjp(lambda given: plackett(given, ranking), scores)
    (grad_scores,) = pull(jnp.ones((), jnp.float32))
    grad_chosen = grad_scores[:, None] * weight
    grad_final = jnp.concatenate(
        [
            jnp.sum(grad_chosen * normal, 0),
            jnp.sum(grad_chosen, 0),
            jnp.sum(grad_scores[:, None] * chosen, 0),
        ]
    )
    return (loss, norm_gradient_pass(grad_chosen * gain_vector, normal, scale), grad_final)


def adamw_update(weight, moment, second, average, gradient_value, rate, decay):
    moment_new = BETA_ONE * moment + (1.0 - BETA_ONE) * gradient_value
    second_new = BETA_TWO * second + (1.0 - BETA_TWO) * gradient_value * gradient_value
    moment_hat = moment_new / (1.0 - BETA_ONE**STEP)
    second_hat = second_new / (1.0 - BETA_TWO**STEP)
    weight_new = weight - rate * (moment_hat / (jnp.sqrt(second_hat) + ADAM_EPS) + decay * weight)
    average_new = EMA_KEEP * average + (1.0 - EMA_KEEP) * weight_new
    return (weight_new, moment_new, second_new, average_new)


def body(
    token_ids,
    seg_lengths,
    rankings,
    table,
    table_m,
    table_v,
    table_ema,
    in_w,
    in_m,
    in_v,
    in_ema,
    out_w,
    out_m,
    out_v,
    out_ema,
    layer_vec,
    vec_m,
    vec_v,
    vec_ema,
    final_vec,
    final_m,
    final_v,
    final_ema,
):
    links = Links()
    core, place, count = links.core, links.dp, links.count
    micro, width = token_ids.shape
    mine_first = core == 0

    own_vec, own_final = lax.reduce_precision(layer_vec[0], 8, 7), lax.reduce_precision(final_vec, 8, 7)
    vec_part, final_part = own_vec.shape[0], own_final.shape[0]
    small = collect_small(
        links, jnp.concatenate([own_vec, own_final, token_ids.astype(jnp.float32).reshape(-1)])
    )
    small_other = links.swap(small[:, :vec_part])
    own_layer, other_layer = small[:, :vec_part].reshape(-1), small_other.reshape(-1)
    vector_0 = jnp.where(mine_first, own_layer, other_layer)
    vector_1 = jnp.where(mine_first, other_layer, own_layer)
    final = small[:, vec_part : vec_part + final_part].reshape(-1)
    every_ids = small[:, vec_part + final_part :].astype(jnp.int32).reshape(count, micro, width)

    low_in, low_out = in_w[0].astype(jnp.bfloat16), out_w[0].astype(jnp.bfloat16)

    def halves(shard):
        rows = shard.shape[0] // 2
        keep = lax.dynamic_slice_in_dim(shard, core * rows, rows, 0)
        give = lax.dynamic_slice_in_dim(shard, (1 - core) * rows, rows, 0)
        got = links.swap(give)
        return (jnp.where(mine_first, keep, got), jnp.where(mine_first, got, keep))

    in_0, in_1 = halves(low_in)
    out_0, out_1 = halves(low_out)
    w_qkv_0 = collect_layers_first(links, in_0[:, : 3 * D])
    w_up_0 = collect_layers_first(links, in_0[:, 3 * D :])
    w_out_0 = collect_layers_first(links, out_0)
    w_qkv_1 = collect_layers_first(links, in_1[:, : 3 * D])
    w_out_1 = collect_layers_last(links, out_1)
    w_up_1 = collect_layers_first(links, in_1[:, 3 * D :])

    ids_here = lax.dynamic_slice_in_dim(every_ids, core, 1, 1).reshape(-1)
    picked = jnp.take(table, ids_here, axis=1).astype(jnp.bfloat16)
    features = picked.shape[0]
    blocks = picked.reshape(features, count, width).transpose(1, 0, 2)
    state = exchange(links, blocks).reshape(D, width).T.astype(jnp.float32)

    lengths = lax.dynamic_slice_in_dim(seg_lengths, core, 1, 0)[0]
    ranking = lax.dynamic_slice_in_dim(rankings, core, 1, 0)[0]
    position, allowed, last = layout(lengths, width)
    cosine, sine = angles(position)

    state_1, kept = first_layer_forward(state, w_qkv_0, w_up_0, w_out_0, vector_0, cosine, sine, allowed)
    state_1 = lax.reduce_precision(state_1, 8, 7)

    ends = last.shape[0]
    first_gain, first_bias, second_gain, second_bias, bias_qkv, bias_attn, bias_up, bias_down = pieces(vector_1)
    normal, scale = standard_deviation(state_1)
    left = (normal * first_gain + first_bias).astype(jnp.bfloat16)
    pairs = matmul(left, w_qkv_1[:, D:]) + bias_qkv[D:]
    keys = turn(pairs[:, :D].reshape(width, HEADS, HEAD_DIM), cosine, sine, 1.0).astype(jnp.bfloat16)
    values = pairs[:, D:].reshape(width, HEADS, HEAD_DIM).astype(jnp.bfloat16)
    normal_end, scale_end, state_end = normal[last], scale[last], state_1[last]
    cosine_end, sine_end, allowed_end = cosine[last], sine[last], allowed[last]
    left_end = (normal_end * first_gain + first_bias).astype(jnp.bfloat16)
    right_end = (normal_end * second_gain + second_bias).astype(jnp.bfloat16)
    query = matmul(left_end, w_qkv_1[:, :D]) + bias_qkv[:D]
    query = turn(query.reshape(ends, HEADS, HEAD_DIM), cosine_end, sine_end, 1.0).astype(jnp.bfloat16)
    upper = matmul(right_end, w_up_1) + bias_up
    weights = softmax_parts(scores_of(query, keys, allowed_end))
    mixed = (
        jnp.einsum("hqk,khe->qhe", weights.astype(jnp.bfloat16), values, preferred_element_type=jnp.float32)
        .reshape(ends, D)
        .astype(jnp.bfloat16)
    )
    active = jax.nn.gelu(upper, approximate=False).astype(jnp.bfloat16)
    branch = matmul(mixed, w_out_1[:D]) + bias_attn + (matmul(active, w_out_1[D:]) + bias_down)
    loss, grad_end, grad_final = head_pass(state_end + branch, final, ranking)

    low_end = grad_end.astype(jnp.bfloat16)
    grad_mixed = dot_cols(low_end, w_out_1[:D]).astype(jnp.bfloat16).reshape(ends, HEADS, HEAD_DIM)
    grad_upper = (dot_cols(low_end, w_out_1[D:]) * gelu_slope(upper)).astype(jnp.bfloat16)
    grad_query, grad_keys, grad_values = attention_backward(query, keys, values, weights, grad_mixed)
    grad_query = turn(grad_query, cosine_end, sine_end, -1.0).reshape(ends, D).astype(jnp.bfloat16)
    grad_pairs = jnp.concatenate(
        [turn(grad_keys, cosine, sine, -1.0).reshape(width, D), grad_values.reshape(width, D)], 1
    ).astype(jnp.bfloat16)
    back_left = dot_cols(grad_pairs, w_qkv_1[:, D:])
    back_left_end = dot_cols(grad_query, w_qkv_1[:, :D])
    back_right_end = dot_cols(grad_upper, w_up_1)
    sum_end = total_rows(low_end)
    sum_vec_1 = jnp.concatenate(
        [
            jnp.sum(back_left * normal, 0) + jnp.sum(back_left_end * normal_end, 0),
            jnp.sum(back_left, 0) + jnp.sum(back_left_end, 0),
            jnp.sum(back_right_end * normal_end, 0),
            jnp.sum(back_right_end, 0),
            total_rows(grad_query),
            total_rows(grad_pairs),
            sum_end,
            total_rows(grad_upper),
            sum_end,
        ]
    )
    row_index = jnp.arange(width, dtype=jnp.int32)
    extra = back_left_end * first_gain + back_right_end * second_gain
    pulled = back_left * first_gain
    landed = jnp.zeros_like(pulled)
    for end in range(ends):
        here = (row_index == last[end])[:, None]
        pulled = pulled + jnp.where(here, extra[end][None], 0.0)
        landed = landed + jnp.where(here, grad_end[end][None], 0.0)
    grad_state = landed + norm_gradient_pass(pulled, normal, scale)
    grad_state = lax.reduce_precision(grad_state, 8, 7).astype(jnp.bfloat16)

    pair_half = reduce_layers_first(links, relative_rows(links, left), grad_pairs)
    factors = jnp.concatenate([left_end, right_end, mixed, active, grad_query, grad_upper, low_end], 1)
    every_factor = collect_layers_first(links, factors)
    in_rows, out_rows = in_w.shape[1], out_w.shape[1]

    def factor_part(begin, size):
        return every_factor[:, begin : begin + size]

    left_own = lax.dynamic_slice_in_dim(factor_part(0, D), place * in_rows, in_rows, 1)
    right_own = lax.dynamic_slice_in_dim(factor_part(D, D), place * in_rows, in_rows, 1)
    acts_own = lax.dynamic_slice_in_dim(factor_part(2 * D, D + FF), place * out_rows, out_rows, 1)
    query_part = factor_part(3 * D + FF, D)
    upper_part = factor_part(4 * D + FF, FF)
    end_part = factor_part(4 * D + 2 * FF, D)
    grad_in_query = dot_rows(left_own, query_part)
    grad_in_upper = dot_rows(right_own, upper_part)
    grad_out_1 = dot_rows(acts_own, end_part)

    normal, scale, left, right, upper, query, keys, values, weights, acts = kept
    first_gain, first_bias, second_gain, second_bias = pieces(vector_0)[:4]
    low_state = grad_state
    acts_relative = relative_rows(links, acts)
    out_half = jnp.concatenate(
        [
            reduce_layers_last(links, acts_relative, low_state[:, : D // 2]),
            reduce_layers_first(links, acts_relative, low_state[:, D // 2 :]),
        ],
        1,
    )
    grad_mixed = dot_cols(low_state, w_out_0[:D]).astype(jnp.bfloat16).reshape(width, HEADS, HEAD_DIM)
    grad_upper = (dot_cols(low_state, w_out_0[D:]) * gelu_slope(upper)).astype(jnp.bfloat16)
    up_half = reduce_layers_first(links, relative_rows(links, right), grad_upper)
    grad_query, grad_keys, grad_values = attention_backward(query, keys, values, weights, grad_mixed)
    grad_joined = jnp.concatenate(
        [
            turn(grad_query, cosine, sine, -1.0).reshape(width, D),
            turn(grad_keys, cosine, sine, -1.0).reshape(width, D),
            grad_values.reshape(width, D),
        ],
        1,
    ).astype(jnp.bfloat16)
    back_left = dot_cols(grad_joined, w_qkv_0)
    back_right = dot_cols(grad_upper, w_up_0)
    sum_state = total_rows(low_state)
    sum_vec_0 = jnp.concatenate(
        [
            jnp.sum(back_left * normal, 0),
            jnp.sum(back_left, 0),
            jnp.sum(back_right * normal, 0),
            jnp.sum(back_right, 0),
            total_rows(grad_joined),
            sum_state,
            total_rows(grad_upper),
            sum_state,
        ]
    )
    grad_embedded = low_state.astype(jnp.float32) + norm_gradient_pass(
        back_left * first_gain + back_right * second_gain, normal, scale
    )
    qkv_half = reduce_layers_first(links, relative_rows(links, left), grad_joined)

    blocks = grad_embedded.astype(jnp.bfloat16).T.reshape(count, features, width)
    spread_mine = exchange(links, blocks).transpose(1, 0, 2)
    spread_other = links.swap(spread_mine)
    spread = jnp.stack(
        [jnp.where(mine_first, spread_mine, spread_other), jnp.where(mine_first, spread_other, spread_mine)], 2
    ).reshape(features, count * micro * width)
    table_grad = jnp.zeros(table.shape, jnp.float32).at[:, every_ids.reshape(-1)].add(spread.astype(jnp.float32))

    packed = jnp.concatenate([sum_vec_0, sum_vec_1, grad_final, loss[None], jnp.zeros((127,), jnp.float32)])
    packed = all_sum(links, packed.reshape(-1, 128)).reshape(-1)
    vec_size = sum_vec_0.shape[0]
    shard_vec = lax.dynamic_slice_in_dim(packed, core * vec_size + place * vec_part, vec_part, 0)
    shard_fin = lax.dynamic_slice_in_dim(packed, 2 * vec_size + place * final_part, final_part, 0)
    loss_sum = packed[2 * vec_size + 3 * D]

    in_half = jnp.concatenate([qkv_half, up_half], 1)
    in_other, out_other, pair_other = links.swap(in_half), links.swap(out_half), links.swap(pair_half)
    grad_in_0 = jnp.concatenate([in_half, in_other], 0)
    grad_out_0 = jnp.concatenate([out_half, out_other], 0)
    grad_in_1 = jnp.concatenate(
        [grad_in_query, jnp.concatenate([pair_other, pair_half], 0), grad_in_upper], 1
    )
    shard_in = jnp.where(mine_first, grad_in_0, grad_in_1)
    shard_out = jnp.where(mine_first, grad_out_0, grad_out_1)

    squares = (
        jnp.sum(shard_in * shard_in)
        + jnp.sum(shard_out * shard_out)
        + jnp.sum(shard_vec * shard_vec)
        + jnp.where(mine_first, jnp.sum(table_grad * table_grad) + jnp.sum(shard_fin * shard_fin), 0.0)
    )
    total_squares = all_sum(links, jnp.broadcast_to(squares, (8, 128)))[0, 0]
    grad_norm = jnp.sqrt(total_squares)
    factor = jnp.minimum(1.0, CLIP_NORM / (grad_norm + 1e-06))
    table_parts = adamw_update(table, table_m, table_v, table_ema, table_grad * factor, RATE_MAT, WEIGHT_DECAY)
    in_parts = adamw_update(
        in_w, in_m, in_v, in_ema, shard_in.reshape(in_w.shape) * factor, RATE_MAT, WEIGHT_DECAY
    )
    out_parts = adamw_update(
        out_w, out_m, out_v, out_ema, shard_out.reshape(out_w.shape) * factor, RATE_MAT, WEIGHT_DECAY
    )
    vec_parts = adamw_update(
        layer_vec, vec_m, vec_v, vec_ema, shard_vec.reshape(layer_vec.shape) * factor, RATE_VEC, 0.0
    )
    final_parts = adamw_update(final_vec, final_m, final_v, final_ema, shard_fin * factor, RATE_VEC, 0.0)
    return (loss_sum, grad_norm) + table_parts + in_parts + out_parts + vec_parts + final_parts


def solution(mesh):
    in_specs = (
        P("dp", None),
        P("dp", None),
        P("dp", None),
        P("dp", None),
        P("dp", None),
        P("dp", None),
        P("dp", None),
        P("section", "dp", None),
        P("section", "dp", None),
        P("section", "dp", None),
        P("section", "dp", None),
        P("section", "dp", None),
        P("section", "dp", None),
        P("section", "dp", None),
        P("section", "dp", None),
        P("section", "dp"),
        P("section", "dp"),
        P("section", "dp"),
        P("section", "dp"),
        P("dp"),
        P("dp"),
        P("dp"),
        P("dp"),
    )
    out_specs = (
        P(),
        P(),
        P("dp", None),
        P("dp", None),
        P("dp", None),
        P("dp", None),
        P("section", "dp", None),
        P("section", "dp", None),
        P("section", "dp", None),
        P("section", "dp", None),
        P("section", "dp", None),
        P("section", "dp", None),
        P("section", "dp", None),
        P("section", "dp", None),
        P("section", "dp"),
        P("section", "dp"),
        P("section", "dp"),
        P("section", "dp"),
        P("dp"),
        P("dp"),
        P("dp"),
        P("dp"),
    )
    return jax.shard_map(body, mesh=mesh, in_specs=in_specs, out_specs=out_specs, check_vma=False)
```

```python
import jax
import jax.numpy as jnp
from jax import lax
from jax.experimental import pallas as pl
from jax.experimental.pallas import tpu as pltpu
from jax.sharding import PartitionSpec as P

D = 1024
HEADS = 16
HEAD_DIM = 64
FF = 4096
ROT = 16
STEP = 10


EPS_NORM = 1e-05
CLIP_NORM = 0.05
BETA_ONE = 0.9
BETA_TWO = 0.95
ADAM_EPS = 1e-08
RATE_MAT = 0.1
RATE_VEC = 0.3
WEIGHT_DECAY = 0.1
EMA_KEEP = 0.75
MASKED = -1e30


def matmul(left_operand, right_operand):
    return jnp.dot(left_operand, right_operand, preferred_element_type=jnp.float32)


def dot_rows(left_operand, right_operand):
    return lax.dot_general(
        left_operand, right_operand, (((0,), (0,)), ((), ())), preferred_element_type=jnp.float32
    )


def dot_cols(left_operand, right_operand):
    return lax.dot_general(
        left_operand, right_operand, (((1,), (1,)), ((), ())), preferred_element_type=jnp.float32
    )


def standard_deviation(value_rows):
    center = value_rows - jnp.mean(value_rows, -1, keepdims=True)
    scale_factor = lax.rsqrt(jnp.mean(center * center, -1, keepdims=True) + EPS_NORM)
    return (center * scale_factor, scale_factor)


def norm_gradient_pass(gradient_normalized, input_normalized, scale_factor):
    return scale_factor * (
        gradient_normalized
        - jnp.mean(gradient_normalized, -1, keepdims=True)
        - input_normalized * jnp.mean(gradient_normalized * input_normalized, -1, keepdims=True)
    )


def layout(lengths, width):
    bounds = jnp.cumsum(lengths)
    starts = bounds - lengths
    places = jnp.arange(width, dtype=jnp.int32)
    segment = jnp.sum((places[:, None] >= bounds[None, :]).astype(jnp.int32), 1)
    pieces_count = lengths.shape[0]
    owner = jnp.minimum(segment, pieces_count - 1)
    chosen = jnp.arange(pieces_count, dtype=jnp.int32)[None, :] == owner[:, None]
    begin = jnp.sum(jnp.where(chosen, starts[None, :], 0), 1)
    position = places - begin + jnp.where(segment > 0, lengths[0], 0)
    same = (segment[:, None] == segment[None, :]) & (places[None, :] <= places[:, None])
    prompt = (segment[None, :] == 0) & (segment[:, None] > 0) & (segment[:, None] < pieces_count)
    return (position, same | prompt, bounds[1:] - 1)


def angles(position):
    half = ROT // 2
    freqs = 10000.0 ** (-2.0 * jnp.arange(half, dtype=jnp.float32) / ROT)
    phase = position.astype(jnp.float32)[:, None] * freqs[None, :]
    return (jnp.cos(phase)[:, None, :], jnp.sin(phase)[:, None, :])


def turn(value_rows, cosine, sine, sign):
    half = cosine.shape[-1]
    first = value_rows[..., :half]
    second = value_rows[..., half : 2 * half]
    return jnp.concatenate(
        [
            first * cosine - sign * second * sine,
            second * cosine + sign * first * sine,
            value_rows[..., 2 * half :],
        ],
        -1,
    )


def pieces(vector):
    amounts = [D, D, D, D, 3 * D, D, FF, D]
    parts = []
    offset = 0
    for amount in amounts:
        parts.append(vector[offset : offset + amount])
        offset = offset + amount
    return parts


def gelu_slope(value_rows):
    cumulative = 0.5 * (1.0 + jax.scipy.special.erf(value_rows * 0.7071067811865476))
    return cumulative + value_rows * jnp.exp(-0.5 * value_rows * value_rows) * 0.3989422804014327


def scores_of(query_rows, key_rows, allowed):
    raw = jnp.einsum(
        "qhe,khe->hqk", query_rows, key_rows, preferred_element_type=jnp.float32
    ) * HEAD_DIM ** (-0.5)
    return jnp.where(allowed[None], raw, MASKED)


def grid(count):
    return {16: (4, 2, 2), 128: (8, 4, 4)}.get(count, (count, 1, 1))


class Links:
    def __init__(self):
        self.count = lax.axis_size("dp")
        self.sizes = grid(self.count)
        self.nz, self.n1, self.n2 = self.sizes
        self.core = lax.axis_index("section")
        self.dp = lax.axis_index("dp")
        self.z = self.dp // (self.n1 * self.n2)
        self.i1 = self.dp // self.n2 % self.n1
        self.i2 = self.dp % self.n2
        self.twist = self.n1 == self.n2
        self.na, self.nb = self.n2, self.n1

    def axis_of(self, kind, core):
        if kind == "z":
            return 0
        if kind == "a":
            return 1 if core == 1 and self.twist else 2
        if kind == "b":
            return 2 if core == 1 and self.twist else 1
        return kind

    def pairs(self, kind, target):
        result = []
        for core in range(2):
            axis = self.axis_of(kind, core)
            for place in range(self.count):
                spot = [place // (self.n1 * self.n2), place // self.n2 % self.n1, place % self.n2]
                spot[axis] = target(spot[axis], self.sizes[axis])
                to = (spot[0] * self.n1 + spot[1]) * self.n2 + spot[2]
                result.append((core * self.count + place, core * self.count + to))
        return result

    def shift(self, value, kind, steps=1):
        pairs = self.pairs(kind, lambda place, size: (place + steps) % size)
        return lax.ppermute(value, ("section", "dp"), pairs)

    def flip(self, value, kind, bit):
        return lax.ppermute(value, ("section", "dp"), self.pairs(kind, lambda place, size: place ^ bit))

    def swap(self, value):
        return lax.ppermute(value, "section", [(0, 1), (1, 0)])

    def plane(self, back_a, back_b, core):
        first = (self.i1 - back_b) % self.n1
        second = (self.i2 - back_a) % self.n2
        usual = first * self.n2 + second
        if not self.twist:
            return usual
        other = (self.i1 - back_a) % self.n1 * self.n2 + (self.i2 - back_b) % self.n2
        return jnp.where(core == 0, usual, other)


def nothing(*refs):
    pass


def blank(shape, kind, after):
    return pl.pallas_call(
        nothing,
        out_shape=jax.ShapeDtypeStruct(shape, kind),
        in_specs=[pl.BlockSpec(memory_space=pl.ANY)] * len(after),
        out_specs=pl.BlockSpec(memory_space=pl.ANY),
        name="blank",
    )(*after)


def behind(value, *after):
    return pl.pallas_call(
        nothing,
        out_shape=jax.ShapeDtypeStruct(value.shape, value.dtype),
        in_specs=[pl.BlockSpec(memory_space=pl.ANY)] * (1 + len(after)),
        out_specs=pl.BlockSpec(memory_space=pl.ANY),
        input_output_aliases={0: 0},
        name="behind",
    )(value, *after)


def update(whole, part, starts):
    starts = [jnp.asarray(start, jnp.int32) for start in starts]
    starts = starts + [jnp.zeros((), jnp.int32)] * (whole.ndim - len(starts))
    return lax.dynamic_update_slice(whole, part, starts)


def place(whole, parts, axis):
    count = len(parts)
    spots = jnp.stack([jnp.asarray(spot, jnp.int32) for _, *pair in parts for spot in pair])
    fresh = isinstance(whole, tuple)
    kind, shape = parts[0][0].dtype, whole if fresh else whole.shape

    def kernel(spots_ref, *refs):
        sources, target, arrived, left = refs[:count], refs[-3 - count], refs[-2], refs[-1]
        buffers = refs[-2 - count : -2]
        loads = [
            pltpu.make_async_copy(sources[at], buffers[at], arrived.at[at]) for at in range(count)
        ]
        stores = []
        for at in range(count):
            spot, half = spots_ref[2 * at], spots_ref[2 * at + 1]
            into = target.at[:, spot, half] if axis == 1 else target.at[spot, :, half]
            stores.append(pltpu.make_async_copy(buffers[at], into, left.at[at]))
        for load in loads:
            load.start()
        for load, store in zip(loads, stores):
            load.wait()
            store.start()
        for store in stores:
            store.wait()

    return pl.pallas_call(
        kernel,
        out_shape=jax.ShapeDtypeStruct(shape, kind),
        grid_spec=pltpu.PrefetchScalarGridSpec(
            num_scalar_prefetch=1,
            grid=(1,),
            in_specs=[pl.BlockSpec(memory_space=pl.ANY)] * (count + (0 if fresh else 1)),
            out_specs=pl.BlockSpec(memory_space=pl.ANY),
            scratch_shapes=[pltpu.VMEM(part.shape, kind) for part, *_ in parts]
            + [pltpu.SemaphoreType.DMA((count,)), pltpu.SemaphoreType.DMA((count,))],
        ),
        input_output_aliases={} if fresh else {1 + count: 0},
        compiler_params=pltpu.CompilerParams(vmem_limit_bytes=40 * 1024 * 1024),
        name="place",
    )(spots, *[part for part, *_ in parts], *([] if fresh else [whole]))


def peek(value):
    ends = [min(size, limit) for size, limit in zip(value.shape[-2:], (8, 128))]
    return lax.slice(value, (0,) * value.ndim, (1,) * (value.ndim - 2) + tuple(ends))


class Pace:
    def __init__(self):
        self.token = None

    def tie(self, value):
        return value if self.token is None else behind(value, self.token)

    def close(self, *values, hold=()):
        hold = [gather for gather in hold if gather.write() is not None]
        held = [gather.buffer for gather in hold]
        taken = len(values) + len(held)

        def kernel(*refs):
            refs[taken][...] = jnp.zeros_like(refs[taken])

        outs = pl.pallas_call(
            kernel,
            out_shape=[jax.ShapeDtypeStruct((8, 128), jnp.float32)]
            + [jax.ShapeDtypeStruct(value.shape, value.dtype) for value in held],
            in_specs=[pl.BlockSpec(memory_space=pl.ANY)] * taken,
            out_specs=[pl.BlockSpec(memory_space=pltpu.VMEM)]
            + [pl.BlockSpec(memory_space=pl.ANY)] * len(held),
            input_output_aliases={len(values) + at: 1 + at for at in range(len(held))},
            name="close",
        )(*values, *held)
        self.token = outs[0]
        for gather, value in zip(hold, outs[1:]):
            gather.buffer = value


class Gather:
    def __init__(self, links, shard):
        self.links, self.piece, self.step, self.level = links, shard, 0, 0
        self.column = blank((links.nz,) + shard.shape, shard.dtype, (shard,))
        self.column = update(self.column, shard[None], [links.z])
        self.found, self.sibling, self.buffer, self.written = None, {}, None, set()

    def along(self, pace, steps=None):
        links, fresh = self.links, []
        self.piece = pace.tie(self.piece)
        while self.step < links.nz - 1 and (steps is None or steps > 0):
            self.step = self.step + 1
            self.piece = links.shift(self.piece, "z")
            self.column = update(self.column, self.piece[None], [(links.z - self.step) % links.nz])
            fresh.append(self.piece)
            steps = None if steps is None else steps - 1
        return fresh

    def wave(self, pace, siblings=True):
        links, fresh = self.links, []
        if self.found is None:
            fresh = self.along(pace)
            self.found = {(0, 0): self.column}
        for key in [key for key in self.found if sum(key) == self.level]:
            self.found[key] = pace.tie(self.found[key])
            if siblings:
                self.sibling[key] = links.swap(self.found[key])
                fresh.append(self.sibling[key])
        self.level = self.level + 1
        for back_a in range(links.na):
            back_b = self.level - back_a
            if 0 <= back_b < links.nb:
                if back_b > 0:
                    value = links.shift(self.found[back_a, back_b - 1], "b")
                else:
                    value = links.shift(self.found[back_a - 1, 0], "a")
                self.found[back_a, back_b] = value
                fresh.append(value)
        return fresh

    def last(self, pace):
        links, fresh = self.links, []
        while self.level < links.na + links.nb - 2:
            fresh = fresh + self.wave(pace)
        for key in self.found:
            if key not in self.sibling:
                self.found[key] = pace.tie(self.found[key])
                self.sibling[key] = links.swap(self.found[key])
                fresh.append(self.sibling[key])
        return fresh

    def write(self):
        links, parts = self.links, []
        nz, rows, width = self.column.shape
        for key in self.sibling:
            if key not in self.written:
                self.written.add(key)
                mine = links.plane(key[0], key[1], links.core)
                theirs = links.plane(key[0], key[1], 1 - links.core)
                parts.append((self.found[key], mine, links.core))
                parts.append((self.sibling[key], theirs, 1 - links.core))
        if parts:
            shape = (nz, links.na * links.nb, 2, rows, width)
            self.buffer = place(shape if self.buffer is None else self.buffer, parts, 1)
        return self.buffer

    def whole(self):
        return self.write().reshape(-1, self.column.shape[2])


class Small:
    def __init__(self, links, row):
        self.links, self.pieces, self.level, self.found = links, [row], 0, None

    def along(self, pace, steps=1):
        while len(self.pieces) < self.links.nz and steps > 0:
            self.pieces.append(self.links.shift(pace.tie(self.pieces[-1]), "z"))
            steps = steps - 1
        return self.pieces[-1:]

    def wave(self, pace):
        links, fresh = self.links, []
        if self.found is None:
            self.along(pace, links.nz)
            self.found = {(0, 0): jnp.stack(self.pieces)}
        for key in [key for key in self.found if sum(key) == self.level]:
            self.found[key] = pace.tie(self.found[key])
        self.level = self.level + 1
        for back_a in range(links.na):
            back_b = self.level - back_a
            if 0 <= back_b < links.nb:
                if back_b > 0:
                    value = links.shift(self.found[back_a, back_b - 1], "b")
                else:
                    value = links.shift(self.found[back_a - 1, 0], "a")
                self.found[back_a, back_b] = value
                fresh.append(value)
        return fresh

    def whole(self, pace):
        links = self.links
        while self.found is None or self.level < links.na + links.nb - 2:
            self.wave(pace)
        parts, places = [], []
        for (back_a, back_b), value in self.found.items():
            parts.append(value)
            plane = links.plane(back_a, back_b, links.core)
            for step in range(links.nz):
                places.append((links.z - step) % links.nz * (links.n1 * links.n2) + plane)
        return place_rows(jnp.concatenate(parts), jnp.stack(places))


def place_rows(found, places):
    count = found.shape[0]
    result = jnp.zeros_like(found)
    spots = jnp.arange(count, dtype=jnp.int32)
    for index in range(count):
        chosen = spots == places[index]
        result = jnp.where(chosen[(slice(None),) + (None,) * (found.ndim - 1)], found[index][None], result)
    return result


def roll_to(value, axis, first):
    size = value.shape[axis]
    if size == 1:
        return value
    doubled = jnp.concatenate([value, value], axis)
    return lax.dynamic_slice_in_dim(doubled, first, size, axis)


def relative_rows(links, left):
    features = left.shape[1]
    nz, n1, n2 = links.sizes
    half = features // (links.count * 2)
    turned = left.T.reshape(nz, n1, n2, 2, half, left.shape[0])
    turned = roll_to(roll_to(roll_to(turned, 0, links.z), 1, links.i1), 2, links.i2)
    turned = roll_to(turned, 3, links.core)
    ordinary = turned.transpose(3, 1, 2, 0, 4, 5)
    if not links.twist:
        return ordinary
    other = turned.transpose(3, 2, 1, 0, 4, 5)
    return jnp.stack(
        [jnp.where(links.core == 0, ordinary[0], other[0]), jnp.where(links.core == 0, other[1], ordinary[1])]
    )


def both_rows(links, left):
    return jnp.concatenate([left[0], links.swap(left[1])], 4)


def halves_total(left, right):
    total = matmul(left.reshape(-1, left.shape[4]), right).astype(jnp.bfloat16)
    return total.reshape(left.shape[:4] + (right.shape[1],))


class Reduce:
    def __init__(self, links, value, kinds):
        self.links, self.value, self.kinds = links, value, list(kinds)
        self.spot, self.moving = value.shape[0] - 1, value[value.shape[0] - 1]

    def step(self, pace, steps=1):
        if not self.kinds:
            return []
        if self.spot == 0:
            self.kinds = self.kinds[1:]
            if not self.kinds:
                return []
            self.value = self.moving
            self.spot, self.moving = self.value.shape[0] - 1, self.value[self.value.shape[0] - 1]
        self.moving = pace.tie(self.moving)
        while self.spot > 0 and steps > 0:
            moved = self.links.shift(self.moving, self.kinds[0])
            self.spot, steps = self.spot - 1, steps - 1
            self.moving = self.value[self.spot].astype(jnp.float32) + moved.astype(jnp.float32)
            if self.spot > 0 or len(self.kinds) > 1:
                self.moving = self.moving.astype(jnp.bfloat16)
        return [self.moving]

    def ring(self, pace):
        return self.step(pace, 1000)

    def done(self, pace):
        while len(self.kinds) > 1 or (self.kinds and self.spot > 0):
            self.ring(pace)
        return self.moving.astype(jnp.float32)


def exchange_along(links, blocks, axis):
    here = (links.z, links.i1, links.i2)[axis]
    size, fresh = links.sizes[axis], blocks
    for steps in range(1, size):
        part = lax.dynamic_slice_in_dim(blocks, (here + steps) % size, 1, axis)
        moved = links.shift(part, axis, steps)
        fresh = lax.dynamic_update_slice_in_dim(fresh, moved, (here - steps) % size, axis)
    return fresh


class Total:
    def __init__(self, links, value):
        self.links, self.value, self.ways = links, value, [None]
        for axis in (2, 1, 0):
            bit = 1
            while bit < links.sizes[axis]:
                self.ways.append((axis, bit))
                bit = bit * 2

    def step(self, pace):
        if self.ways:
            way, self.ways = self.ways[0], self.ways[1:]
            self.value = pace.tie(self.value)
            moved = self.links.swap(self.value) if way is None else self.links.flip(self.value, *way)
            self.value = self.value + moved
        return [self.value]

    def done(self, pace):
        while self.ways:
            self.step(pace)
        return self.value


def all_sum(links, value):
    value = value + links.swap(value)
    for axis in (2, 1, 0):
        bit = 1
        while bit < links.sizes[axis]:
            value = value + links.flip(value, axis, bit)
            bit = bit * 2
    return value


def softmax_parts(scores):
    top_score = jnp.max(scores, -1, keepdims=True)
    powers = jnp.exp(scores - top_score)
    return powers / jnp.sum(powers, -1, keepdims=True)


def attention_backward(query, keys, values, weights, grad_mixed):
    factor = HEAD_DIM ** (-0.5)
    grad_weights = jnp.einsum("qhe,khe->hqk", grad_mixed, values, preferred_element_type=jnp.float32)
    grad_scores = (weights * (grad_weights - jnp.sum(weights * grad_weights, -1, keepdims=True))).astype(jnp.bfloat16)
    grad_values = jnp.einsum(
        "hqk,qhe->khe", weights.astype(jnp.bfloat16), grad_mixed, preferred_element_type=jnp.float32
    )
    grad_query = jnp.einsum("hqk,khe->qhe", grad_scores, keys, preferred_element_type=jnp.float32) * factor
    grad_keys = jnp.einsum("hqk,qhe->khe", grad_scores, query, preferred_element_type=jnp.float32) * factor
    return (grad_query, grad_keys, grad_values)


def total_rows(value):
    return jnp.sum(value.astype(jnp.float32), 0)


def plackett(scores, ranking):
    ordered = scores[ranking]
    count = ordered.shape[0]
    later = jnp.arange(count)[None, :] >= jnp.arange(count)[:, None]
    grid = jnp.where(later, ordered[None, :], MASKED)
    top_score = jnp.max(grid, 1, keepdims=True)
    tails = top_score[:, 0] + jnp.log(jnp.sum(jnp.exp(grid - top_score), 1))
    return jnp.sum(tails - ordered)


def head_pass(state, final, ranking):
    gain_vector, bias_vector, weight = (final[:D], final[D : 2 * D], final[2 * D :])
    normal, scale = standard_deviation(state)
    chosen = lax.reduce_precision(normal * gain_vector + bias_vector, 8, 7)
    scores = jnp.sum(chosen * weight, -1)
    loss, pull = jax.vjp(lambda given: plackett(given, ranking), scores)
    (grad_scores,) = pull(jnp.ones((), jnp.float32))
    grad_chosen = grad_scores[:, None] * weight
    grad_final = jnp.concatenate(
        [
            jnp.sum(grad_chosen * normal, 0),
            jnp.sum(grad_chosen, 0),
            jnp.sum(grad_scores[:, None] * chosen, 0),
        ]
    )
    return (loss, norm_gradient_pass(grad_chosen * gain_vector, normal, scale), grad_final)


def adamw_update(weight, moment, second, average, gradient_value, rate, decay):
    moment_new = BETA_ONE * moment + (1.0 - BETA_ONE) * gradient_value
    second_new = BETA_TWO * second + (1.0 - BETA_TWO) * gradient_value * gradient_value
    moment_hat = moment_new / (1.0 - BETA_ONE**STEP)
    second_hat = second_new / (1.0 - BETA_TWO**STEP)
    weight_new = weight - rate * (moment_hat / (jnp.sqrt(second_hat) + ADAM_EPS) + decay * weight)
    average_new = EMA_KEEP * average + (1.0 - EMA_KEEP) * weight_new
    return (weight_new, moment_new, second_new, average_new)


def low_rows(table, token):
    features, vocabulary = table.shape
    block = 4096

    def kernel(table_ref, token_ref, out_ref):
        out_ref[...] = table_ref[...].T.astype(jnp.bfloat16)

    return pl.pallas_call(
        kernel,
        grid=(pl.cdiv(vocabulary, block),),
        out_shape=jax.ShapeDtypeStruct((vocabulary, features), jnp.bfloat16),
        in_specs=[
            pl.BlockSpec((features, block), lambda at: (0, at)),
            pl.BlockSpec(memory_space=pl.ANY),
        ],
        out_specs=pl.BlockSpec((block, features), lambda at: (at, 0)),
        compiler_params=pltpu.CompilerParams(vmem_limit_bytes=48 * 1024 * 1024),
        name="low_rows",
    )(table, token)


def sum_rows(ids, rows, count):
    tokens, features = rows.shape
    unroll, block = 32, 64

    def kernel(ids_ref, rows_ref, out_ref, squares_ref):
        def clear(at, carry):
            out_ref[pl.ds(at * block, block), :] = jnp.zeros((block, features), jnp.float32)
            return carry

        lax.fori_loop(0, count // block, clear, 0)

        def add(at, carry):
            for step in range(unroll):
                token = at * unroll + step
                spot = ids_ref[token]
                out_ref[pl.ds(spot, 1), :] = out_ref[pl.ds(spot, 1), :] + rows_ref[pl.ds(token, 1), :]
            return carry

        lax.fori_loop(0, tokens // unroll, add, 0)

        def square(at, total):
            value = out_ref[pl.ds(at * block, block), :]
            return total + jnp.sum((value * value).reshape(block // 8, 8, features), 0)

        total = lax.fori_loop(0, count // block, square, jnp.zeros((8, features), jnp.float32))
        squares_ref[0, 0] = jnp.sum(total)

    summed, squares = pl.pallas_call(
        kernel,
        out_shape=(
            jax.ShapeDtypeStruct((count, features), jnp.float32),
            jax.ShapeDtypeStruct((1, 1), jnp.float32),
        ),
        grid_spec=pltpu.PrefetchScalarGridSpec(
            num_scalar_prefetch=1,
            grid=(1,),
            in_specs=[pl.BlockSpec((tokens, features), lambda at, ids: (0, 0))],
            out_specs=[
                pl.BlockSpec((count, features), lambda at, ids: (0, 0), pipeline_mode=pl.Buffered(1)),
                pl.BlockSpec(memory_space=pltpu.SMEM),
            ],
        ),
        compiler_params=pltpu.CompilerParams(vmem_limit_bytes=58 * 1024 * 1024),
        name="sum_rows",
    )(ids, rows)
    return (summed, squares[0, 0])


def table_update(table, moment, second, average, grad_rows, factor):
    features, vocabulary = table.shape
    block = 2048

    def kernel(factor_ref, table_ref, moment_ref, second_ref, average_ref, grad_ref, *outs):
        grad = grad_ref[...].T * factor_ref[0, 0]
        parts = adamw_update(
            table_ref[...], moment_ref[...], second_ref[...], average_ref[...], grad, RATE_MAT, WEIGHT_DECAY
        )
        for out, part in zip(outs, parts):
            out[...] = part

    wide = pl.BlockSpec((features, block), lambda at: (0, at))
    return tuple(
        pl.pallas_call(
            kernel,
            grid=(pl.cdiv(vocabulary, block),),
            out_shape=[jax.ShapeDtypeStruct(table.shape, jnp.float32)] * 4,
            in_specs=[pl.BlockSpec(memory_space=pltpu.SMEM)]
            + [wide] * 4
            + [pl.BlockSpec((block, features), lambda at: (at, 0))],
            out_specs=[wide] * 4,
            compiler_params=pltpu.CompilerParams(vmem_limit_bytes=48 * 1024 * 1024),
            name="table_update",
        )(factor.reshape(1, 1), table, moment, second, average, grad_rows)
    )


def body(
    token_ids,
    seg_lengths,
    rankings,
    table,
    table_m,
    table_v,
    table_ema,
    in_w,
    in_m,
    in_v,
    in_ema,
    out_w,
    out_m,
    out_v,
    out_ema,
    layer_vec,
    vec_m,
    vec_v,
    vec_ema,
    final_vec,
    final_m,
    final_v,
    final_ema,
):
    links = Links()
    core, place, count = links.core, links.dp, links.count
    micro, width = token_ids.shape
    mine_first = core == 0

    pace = Pace()
    low_in, low_out = in_w[0].astype(jnp.bfloat16), out_w[0].astype(jnp.bfloat16)

    def halves(shard):
        rows = shard.shape[0] // 2
        keep = lax.dynamic_slice_in_dim(shard, core * rows, rows, 0)
        give = lax.dynamic_slice_in_dim(shard, (1 - core) * rows, rows, 0)
        got = links.swap(give)
        return (jnp.where(mine_first, keep, got), jnp.where(mine_first, got, keep))

    in_0, in_1 = halves(low_in)
    out_0, out_1 = halves(low_out)
    own_vec, own_final = lax.reduce_precision(layer_vec[0], 8, 7), lax.reduce_precision(final_vec, 8, 7)
    vec_part, final_part = own_vec.shape[0], own_final.shape[0]
    small = Small(links, jnp.concatenate([own_vec, own_final, token_ids.astype(jnp.float32).reshape(-1)]))
    pace.close(in_0, out_0, *small.along(pace))
    w_in_0 = lax.all_gather(in_0, ("dp", "section"), axis=0, tiled=True)
    w_up_1 = lax.all_gather(in_1[:, 3 * D :], ("dp", "section"), axis=0, tiled=True)
    w_out_1 = lax.all_gather(out_1, ("dp", "section"), axis=0, tiled=True)
    out_0, qkv_1 = Gather(links, out_0), Gather(links, in_1[:, : 3 * D])
    pace.close(*small.along(pace))
    table_rows = low_rows(table, pace.token)
    pace.close(*small.along(pace), peek(table_rows))
    pace.close(*small.wave(pace))
    pace.close(*small.wave(pace))
    lengths = lax.dynamic_slice_in_dim(seg_lengths, core, 1, 0)[0]
    small = small.whole(pace)
    small_other = links.swap(small[:, :vec_part])
    own_layer, other_layer = small[:, :vec_part].reshape(-1), small_other.reshape(-1)
    vector_0 = jnp.where(mine_first, own_layer, other_layer)
    vector_1 = jnp.where(mine_first, other_layer, own_layer)
    final = small[:, vec_part : vec_part + final_part].reshape(-1)
    every_ids = small[:, vec_part + final_part :].astype(jnp.int32).reshape(count, micro, width)

    ids_here = lax.dynamic_slice_in_dim(every_ids, core, 1, 1).reshape(-1)
    picked = jnp.take(table_rows, pace.tie(ids_here), axis=0, mode="clip")
    features = picked.shape[1]
    blocks = picked.reshape(links.sizes + (width, features)).transpose(0, 1, 2, 4, 3)
    pace.close(peek(blocks), *out_0.along(pace, 1))
    blocks = exchange_along(links, pace.tie(blocks), 2)
    pace.close(peek(blocks), *out_0.along(pace, 1))
    blocks = exchange_along(links, pace.tie(blocks), 1)
    pace.close(peek(blocks), *out_0.along(pace))
    blocks = exchange_along(links, pace.tie(blocks), 0)
    pace.close(peek(blocks))
    state = blocks.reshape(D, width).T.astype(jnp.float32)

    ranking = lax.dynamic_slice_in_dim(rankings, core, 1, 0)[0]
    position, allowed, last = layout(lengths, width)
    cosine, sine = angles(position)

    first_gain, first_bias, second_gain, second_bias, bias_qkv, bias_attn, bias_up, bias_down = pieces(vector_0)
    normal, scale = standard_deviation(state)
    left = (normal * first_gain + first_bias).astype(jnp.bfloat16)
    right = (normal * second_gain + second_bias).astype(jnp.bfloat16)
    joined = matmul(pace.tie(left), w_in_0[:, : 3 * D]) + bias_qkv
    query = turn(joined[:, :D].reshape(width, HEADS, HEAD_DIM), cosine, sine, 1.0).astype(jnp.bfloat16)
    keys = turn(joined[:, D : 2 * D].reshape(width, HEADS, HEAD_DIM), cosine, sine, 1.0).astype(jnp.bfloat16)
    values = joined[:, 2 * D :].reshape(width, HEADS, HEAD_DIM).astype(jnp.bfloat16)
    weights = softmax_parts(scores_of(query, keys, allowed))
    mixed = (
        jnp.einsum("hqk,khe->qhe", weights.astype(jnp.bfloat16), values, preferred_element_type=jnp.float32)
        .reshape(width, D)
        .astype(jnp.bfloat16)
    )
    pace.close(*out_0.wave(pace), *qkv_1.along(pace, 1), peek(mixed))
    upper = matmul(pace.tie(right), w_in_0[:, 3 * D :]) + bias_up
    active = jax.nn.gelu(upper, approximate=False).astype(jnp.bfloat16)
    pace.close(*out_0.wave(pace), *qkv_1.along(pace, 1), peek(active))
    left_both = both_rows(links, relative_rows(links, left))
    right_both = both_rows(links, relative_rows(links, right))
    pace.close(*out_0.last(pace), *qkv_1.along(pace), peek(left_both), peek(right_both))
    w_out_0 = out_0.whole()
    acts = jnp.concatenate([mixed, active], 1)
    state_1 = (
        state + matmul(mixed, w_out_0[:D]) + bias_attn + (matmul(pace.tie(active), w_out_0[D:]) + bias_down)
    )
    state_1 = lax.reduce_precision(state_1, 8, 7)
    kept = (normal, scale, left, right, upper, query, keys, values, weights, acts)
    pace.close(*qkv_1.wave(pace), peek(state_1))
    pace.close(*qkv_1.wave(pace))
    pace.close(*qkv_1.last(pace))
    w_qkv_1 = qkv_1.whole()
    state_1 = pace.tie(state_1)

    ends = last.shape[0]
    first_gain, first_bias, second_gain, second_bias, bias_qkv, bias_attn, bias_up, bias_down = pieces(vector_1)
    normal, scale = standard_deviation(state_1)
    left = (normal * first_gain + first_bias).astype(jnp.bfloat16)
    pairs = matmul(left, w_qkv_1[:, D:]) + bias_qkv[D:]
    keys = turn(pairs[:, :D].reshape(width, HEADS, HEAD_DIM), cosine, sine, 1.0).astype(jnp.bfloat16)
    values = pairs[:, D:].reshape(width, HEADS, HEAD_DIM).astype(jnp.bfloat16)
    normal_end, scale_end, state_end = normal[last], scale[last], state_1[last]
    cosine_end, sine_end, allowed_end = cosine[last], sine[last], allowed[last]
    left_end = (normal_end * first_gain + first_bias).astype(jnp.bfloat16)
    right_end = (normal_end * second_gain + second_bias).astype(jnp.bfloat16)
    query = matmul(left_end, w_qkv_1[:, :D]) + bias_qkv[:D]
    query = turn(query.reshape(ends, HEADS, HEAD_DIM), cosine_end, sine_end, 1.0).astype(jnp.bfloat16)
    upper = matmul(right_end, w_up_1) + bias_up
    weights = softmax_parts(scores_of(query, keys, allowed_end))
    mixed = (
        jnp.einsum("hqk,khe->qhe", weights.astype(jnp.bfloat16), values, preferred_element_type=jnp.float32)
        .reshape(ends, D)
        .astype(jnp.bfloat16)
    )
    active = jax.nn.gelu(upper, approximate=False).astype(jnp.bfloat16)
    branch = matmul(mixed, w_out_1[:D]) + bias_attn + (matmul(active, w_out_1[D:]) + bias_down)
    loss, grad_end, grad_final = head_pass(state_end + branch, final, ranking)

    low_end = grad_end.astype(jnp.bfloat16)
    grad_mixed = dot_cols(low_end, w_out_1[:D]).astype(jnp.bfloat16).reshape(ends, HEADS, HEAD_DIM)
    grad_upper = (dot_cols(low_end, w_out_1[D:]) * gelu_slope(upper)).astype(jnp.bfloat16)
    grad_query, grad_keys, grad_values = attention_backward(query, keys, values, weights, grad_mixed)
    grad_query = turn(grad_query, cosine_end, sine_end, -1.0).reshape(ends, D).astype(jnp.bfloat16)
    grad_pairs = jnp.concatenate(
        [turn(grad_keys, cosine, sine, -1.0).reshape(width, D), grad_values.reshape(width, D)], 1
    ).astype(jnp.bfloat16)
    back_left = dot_cols(grad_pairs, w_qkv_1[:, D:])
    back_left_end = dot_cols(grad_query, w_qkv_1[:, :D])
    back_right_end = dot_cols(grad_upper, w_up_1)
    sum_end = total_rows(low_end)
    sum_vec_1 = jnp.concatenate(
        [
            jnp.sum(back_left * normal, 0) + jnp.sum(back_left_end * normal_end, 0),
            jnp.sum(back_left, 0) + jnp.sum(back_left_end, 0),
            jnp.sum(back_right_end * normal_end, 0),
            jnp.sum(back_right_end, 0),
            total_rows(grad_query),
            total_rows(grad_pairs),
            sum_end,
            total_rows(grad_upper),
            sum_end,
        ]
    )
    row_index = jnp.arange(width, dtype=jnp.int32)
    extra = back_left_end * first_gain + back_right_end * second_gain
    pulled = back_left * first_gain
    landed = jnp.zeros_like(pulled)
    for end in range(ends):
        here = (row_index == last[end])[:, None]
        pulled = pulled + jnp.where(here, extra[end][None], 0.0)
        landed = landed + jnp.where(here, grad_end[end][None], 0.0)
    grad_state = landed + norm_gradient_pass(pulled, normal, scale)
    grad_state = lax.reduce_precision(grad_state, 8, 7).astype(jnp.bfloat16)

    pairs_both = both_rows(links, relative_rows(links, left))
    pairs_grad = jnp.concatenate([grad_pairs, links.swap(grad_pairs)])
    factors = jnp.concatenate([left_end, right_end, mixed, active, grad_query, grad_upper, low_end], 1)
    every_factor = lax.all_gather(factors, ("dp", "section"), axis=0, tiled=True)
    in_rows, out_rows = in_w.shape[1], out_w.shape[1]

    normal, scale, left, right, upper, query, keys, values, weights, acts = kept
    first_gain, first_bias, second_gain, second_bias = pieces(vector_0)[:4]
    low_state = grad_state
    pair_sum = Reduce(links, halves_total(pairs_both, pairs_grad), "baz")
    pace.close(peek(pair_sum.moving), peek(low_state))
    low_state = pace.tie(low_state)
    out_half = dot_rows(acts, low_state).astype(jnp.bfloat16)
    out_half = lax.psum_scatter(out_half, ("dp", "section"), scatter_dimension=0, tiled=True)
    grad_mixed = dot_cols(low_state, w_out_0[:D]).astype(jnp.bfloat16).reshape(width, HEADS, HEAD_DIM)
    grad_upper = (dot_cols(low_state, w_out_0[D:]) * gelu_slope(upper)).astype(jnp.bfloat16)
    upper_both = jnp.concatenate([grad_upper, links.swap(grad_upper)])
    pace.close(*map(peek, pair_sum.ring(pace)), peek(grad_mixed), peek(upper_both))
    up_sum = halves_total(right_both, pace.tie(upper_both))
    grad_query, grad_keys, grad_values = attention_backward(query, keys, values, weights, pace.tie(grad_mixed))
    grad_joined = jnp.concatenate(
        [
            turn(grad_query, cosine, sine, -1.0).reshape(width, D),
            turn(grad_keys, cosine, sine, -1.0).reshape(width, D),
            grad_values.reshape(width, D),
        ],
        1,
    ).astype(jnp.bfloat16)
    pace.close(*map(peek, pair_sum.ring(pace)), peek(up_sum), peek(grad_joined))
    up_sum = Reduce(links, up_sum, "baz")
    grad_joined = pace.tie(grad_joined)
    back_left = dot_cols(grad_joined, w_in_0[:, : 3 * D])
    back_right = dot_cols(grad_upper, w_in_0[:, 3 * D :])
    grad_embedded = low_state.astype(jnp.float32) + norm_gradient_pass(
        back_left * first_gain + back_right * second_gain, normal, scale
    )
    joined_both = jnp.concatenate([grad_joined, links.swap(grad_joined)])
    blocks = grad_embedded.astype(jnp.bfloat16).T.reshape(links.sizes + (features, width))
    pace.close(*map(peek, up_sum.ring(pace) + pair_sum.step(pace)), peek(joined_both), peek(blocks))
    blocks = exchange_along(links, pace.tie(blocks), 2)
    qkv_sum = halves_total(left_both, pace.tie(joined_both))
    pace.close(*map(peek, pair_sum.step(pace)), peek(blocks), peek(qkv_sum))
    qkv_sum = Reduce(links, qkv_sum, "baz")
    blocks = exchange_along(links, pace.tie(blocks), 1)
    back_left, back_right = pace.tie(back_left), pace.tie(back_right)
    sum_state = total_rows(low_state)
    sum_vec_0 = jnp.concatenate(
        [
            jnp.sum(back_left * normal, 0),
            jnp.sum(back_left, 0),
            jnp.sum(back_right * normal, 0),
            jnp.sum(back_right, 0),
            total_rows(grad_joined),
            sum_state,
            total_rows(grad_upper),
            sum_state,
        ]
    )
    packed = jnp.concatenate([sum_vec_0, sum_vec_1, grad_final, loss[None], jnp.zeros((127,), jnp.float32)])
    packed = Total(links, packed.reshape(-1, 128))
    pace.close(*map(peek, pair_sum.step(pace)), peek(blocks), packed.value)
    blocks = exchange_along(links, pace.tie(blocks), 0)
    pace.close(*map(peek, up_sum.ring(pace)), peek(blocks), *packed.step(pace))
    blocks = pace.tie(blocks)
    spread_mine = blocks.reshape(count, features, width).transpose(0, 2, 1)
    spread_other = links.swap(spread_mine)
    spread = jnp.stack(
        [jnp.where(mine_first, spread_mine, spread_other), jnp.where(mine_first, spread_other, spread_mine)], 1
    ).reshape(count * micro * width, features)
    table_grad, table_squares = sum_rows(every_ids.reshape(-1), spread.astype(jnp.float32), table.shape[1])
    pace.close(*map(peek, up_sum.step(pace) + qkv_sum.ring(pace)), peek(table_grad))
    pace.close(*map(peek, up_sum.step(pace) + qkv_sum.ring(pace)), *packed.step(pace))
    pace.close(*map(peek, up_sum.ring(pace) + qkv_sum.step(pace)), *packed.step(pace))
    pace.close(*map(peek, qkv_sum.step(pace)), *packed.step(pace))
    pace.close(*map(peek, qkv_sum.ring(pace)), *packed.step(pace))
    up_half, pair_half, qkv_half = up_sum.done(pace), pair_sum.done(pace), qkv_sum.done(pace)
    def factor_part(begin, size):
        return every_factor[:, begin : begin + size]

    left_own = lax.dynamic_slice_in_dim(factor_part(0, D), place * in_rows, in_rows, 1)
    right_own = lax.dynamic_slice_in_dim(factor_part(D, D), place * in_rows, in_rows, 1)
    acts_own = lax.dynamic_slice_in_dim(factor_part(2 * D, D + FF), place * out_rows, out_rows, 1)
    query_part = factor_part(3 * D + FF, D)
    upper_part = factor_part(4 * D + FF, FF)
    end_part = factor_part(4 * D + 2 * FF, D)
    grad_in_query = dot_rows(left_own, query_part)
    grad_in_upper = dot_rows(right_own, upper_part)
    grad_out_1 = dot_rows(acts_own, end_part)


    packed = packed.done(pace).reshape(-1)
    vec_size = sum_vec_0.shape[0]
    shard_vec = lax.dynamic_slice_in_dim(packed, core * vec_size + place * vec_part, vec_part, 0)
    shard_fin = lax.dynamic_slice_in_dim(packed, 2 * vec_size + place * final_part, final_part, 0)
    loss_sum = packed[2 * vec_size + 3 * D]

    in_half = jnp.concatenate([qkv_half, up_half], 1)
    in_other, out_other, pair_other = links.swap(in_half), links.swap(out_half), links.swap(pair_half)
    grad_in_0 = jnp.concatenate([in_half, in_other], 0)
    out_half = out_half.astype(jnp.float32)
    grad_out_0 = jnp.concatenate([out_half, out_other.astype(jnp.float32)], 0)
    grad_in_1 = jnp.concatenate(
        [grad_in_query, jnp.concatenate([pair_other, pair_half], 0), grad_in_upper], 1
    )
    shard_in = jnp.where(mine_first, grad_in_0, grad_in_1)
    shard_out = jnp.where(mine_first, grad_out_0, grad_out_1)

    squares = (
        jnp.sum(shard_in * shard_in)
        + jnp.sum(shard_out * shard_out)
        + jnp.sum(shard_vec * shard_vec)
        + jnp.where(mine_first, table_squares + jnp.sum(shard_fin * shard_fin), 0.0)
    )
    total_squares = all_sum(links, jnp.broadcast_to(squares, (8, 128)))[0, 0]
    grad_norm = jnp.sqrt(total_squares)
    factor = jnp.minimum(1.0, CLIP_NORM / (grad_norm + 1e-06))
    table_parts = table_update(table, table_m, table_v, table_ema, table_grad, factor)
    in_parts = adamw_update(
        in_w, in_m, in_v, in_ema, shard_in.reshape(in_w.shape) * factor, RATE_MAT, WEIGHT_DECAY
    )
    out_parts = adamw_update(
        out_w, out_m, out_v, out_ema, shard_out.reshape(out_w.shape) * factor, RATE_MAT, WEIGHT_DECAY
    )
    vec_parts = adamw_update(
        layer_vec, vec_m, vec_v, vec_ema, shard_vec.reshape(layer_vec.shape) * factor, RATE_VEC, 0.0
    )
    final_parts = adamw_update(final_vec, final_m, final_v, final_ema, shard_fin * factor, RATE_VEC, 0.0)
    return (loss_sum, grad_norm) + table_parts + in_parts + out_parts + vec_parts + final_parts


def solution(mesh):
    in_specs = (
        P("dp", None),
        P("dp", None),
        P("dp", None),
        P("dp", None),
        P("dp", None),
        P("dp", None),
        P("dp", None),
        P("section", "dp", None),
        P("section", "dp", None),
        P("section", "dp", None),
        P("section", "dp", None),
        P("section", "dp", None),
        P("section", "dp", None),
        P("section", "dp", None),
        P("section", "dp", None),
        P("section", "dp"),
        P("section", "dp"),
        P("section", "dp"),
        P("section", "dp"),
        P("dp"),
        P("dp"),
        P("dp"),
        P("dp"),
    )
    out_specs = (
        P(),
        P(),
        P("dp", None),
        P("dp", None),
        P("dp", None),
        P("dp", None),
        P("section", "dp", None),
        P("section", "dp", None),
        P("section", "dp", None),
        P("section", "dp", None),
        P("section", "dp", None),
        P("section", "dp", None),
        P("section", "dp", None),
        P("section", "dp", None),
        P("section", "dp"),
        P("section", "dp"),
        P("section", "dp"),
        P("section", "dp"),
        P("dp"),
        P("dp"),
        P("dp"),
        P("dp"),
    )
    return jax.shard_map(body, mesh=mesh, in_specs=in_specs, out_specs=out_specs, check_vma=False)
```

```python
import jax
import jax.numpy as jnp
from jax import lax
from jax.experimental import pallas as pl
from jax.experimental.pallas import tpu as pltpu
from jax.sharding import PartitionSpec as P

D = 1024
HEADS = 16
HEAD_DIM = 64
FF = 4096
ROT = 16
STEP = 10


EPS_NORM = 1e-05
CLIP_NORM = 0.05
BETA_ONE = 0.9
BETA_TWO = 0.95
ADAM_EPS = 1e-08
RATE_MAT = 0.1
RATE_VEC = 0.3
WEIGHT_DECAY = 0.1
EMA_KEEP = 0.75
MASKED = -1e30


def matmul(left_operand, right_operand):
    return jnp.dot(left_operand, right_operand, preferred_element_type=jnp.float32)


def dot_rows(left_operand, right_operand):
    return lax.dot_general(
        left_operand, right_operand, (((0,), (0,)), ((), ())), preferred_element_type=jnp.float32
    )


def dot_cols(left_operand, right_operand):
    return lax.dot_general(
        left_operand, right_operand, (((1,), (1,)), ((), ())), preferred_element_type=jnp.float32
    )


def standard_deviation(value_rows):
    center = value_rows - jnp.mean(value_rows, -1, keepdims=True)
    scale_factor = lax.rsqrt(jnp.mean(center * center, -1, keepdims=True) + EPS_NORM)
    return (center * scale_factor, scale_factor)


def norm_gradient_pass(gradient_normalized, input_normalized, scale_factor):
    return scale_factor * (
        gradient_normalized
        - jnp.mean(gradient_normalized, -1, keepdims=True)
        - input_normalized * jnp.mean(gradient_normalized * input_normalized, -1, keepdims=True)
    )


def layout(lengths, width):
    bounds = jnp.cumsum(lengths)
    starts = bounds - lengths
    places = jnp.arange(width, dtype=jnp.int32)
    segment = jnp.sum((places[:, None] >= bounds[None, :]).astype(jnp.int32), 1)
    pieces_count = lengths.shape[0]
    owner = jnp.minimum(segment, pieces_count - 1)
    chosen = jnp.arange(pieces_count, dtype=jnp.int32)[None, :] == owner[:, None]
    begin = jnp.sum(jnp.where(chosen, starts[None, :], 0), 1)
    position = places - begin + jnp.where(segment > 0, lengths[0], 0)
    same = (segment[:, None] == segment[None, :]) & (places[None, :] <= places[:, None])
    prompt = (segment[None, :] == 0) & (segment[:, None] > 0) & (segment[:, None] < pieces_count)
    return (position, same | prompt, bounds[1:] - 1)


def angles(position):
    half = ROT // 2
    freqs = 10000.0 ** (-2.0 * jnp.arange(half, dtype=jnp.float32) / ROT)
    phase = position.astype(jnp.float32)[:, None] * freqs[None, :]
    return (jnp.cos(phase)[:, None, :], jnp.sin(phase)[:, None, :])


def turn(value_rows, cosine, sine, sign):
    half = cosine.shape[-1]
    first = value_rows[..., :half]
    second = value_rows[..., half : 2 * half]
    return jnp.concatenate(
        [
            first * cosine - sign * second * sine,
            second * cosine + sign * first * sine,
            value_rows[..., 2 * half :],
        ],
        -1,
    )


def pieces(vector):
    amounts = [D, D, D, D, 3 * D, D, FF, D]
    parts = []
    offset = 0
    for amount in amounts:
        parts.append(vector[offset : offset + amount])
        offset = offset + amount
    return parts


def gelu_slope(value_rows):
    cumulative = 0.5 * (1.0 + jax.scipy.special.erf(value_rows * 0.7071067811865476))
    return cumulative + value_rows * jnp.exp(-0.5 * value_rows * value_rows) * 0.3989422804014327


def scores_of(query_rows, key_rows, allowed):
    raw = jnp.einsum(
        "qhe,khe->hqk", query_rows, key_rows, preferred_element_type=jnp.float32
    ) * HEAD_DIM ** (-0.5)
    return jnp.where(allowed[None], raw, MASKED)


def grid(count):
    return {16: (4, 2, 2), 128: (8, 4, 4)}.get(count, (count, 1, 1))


class Links:
    def __init__(self):
        self.count = lax.axis_size("dp")
        self.sizes = grid(self.count)
        self.nz, self.n1, self.n2 = self.sizes
        self.core = lax.axis_index("section")
        self.dp = lax.axis_index("dp")
        self.z = self.dp // (self.n1 * self.n2)
        self.i1 = self.dp // self.n2 % self.n1
        self.i2 = self.dp % self.n2
        self.twist = self.n1 == self.n2
        self.na, self.nb = self.n2, self.n1

    def axis_of(self, kind, core):
        if kind == "z":
            return 0
        if kind == "a":
            return 1 if core == 1 and self.twist else 2
        if kind == "b":
            return 2 if core == 1 and self.twist else 1
        return kind

    def pairs(self, kind, target):
        result = []
        for core in range(2):
            axis = self.axis_of(kind, core)
            for place in range(self.count):
                spot = [place // (self.n1 * self.n2), place // self.n2 % self.n1, place % self.n2]
                spot[axis] = target(spot[axis], self.sizes[axis])
                to = (spot[0] * self.n1 + spot[1]) * self.n2 + spot[2]
                result.append((core * self.count + place, core * self.count + to))
        return result

    def shift(self, value, kind, steps=1):
        pairs = self.pairs(kind, lambda place, size: (place + steps) % size)
        return lax.ppermute(value, ("section", "dp"), pairs)

    def flip(self, value, kind, bit):
        return lax.ppermute(value, ("section", "dp"), self.pairs(kind, lambda place, size: place ^ bit))

    def swap(self, value):
        return lax.ppermute(value, "section", [(0, 1), (1, 0)])

    def plane(self, back_a, back_b, core):
        first = (self.i1 - back_b) % self.n1
        second = (self.i2 - back_a) % self.n2
        usual = first * self.n2 + second
        if not self.twist:
            return usual
        other = (self.i1 - back_a) % self.n1 * self.n2 + (self.i2 - back_b) % self.n2
        return jnp.where(core == 0, usual, other)


def nothing(*refs):
    pass


def blank(shape, kind, after):
    return pl.pallas_call(
        nothing,
        out_shape=jax.ShapeDtypeStruct(shape, kind),
        in_specs=[pl.BlockSpec(memory_space=pl.ANY)] * len(after),
        out_specs=pl.BlockSpec(memory_space=pl.ANY),
        name="blank",
    )(*after)


def behind(value, *after):
    return pl.pallas_call(
        nothing,
        out_shape=jax.ShapeDtypeStruct(value.shape, value.dtype),
        in_specs=[pl.BlockSpec(memory_space=pl.ANY)] * (1 + len(after)),
        out_specs=pl.BlockSpec(memory_space=pl.ANY),
        input_output_aliases={0: 0},
        name="behind",
    )(value, *after)


def update(whole, part, starts):
    starts = [jnp.asarray(start, jnp.int32) for start in starts]
    starts = starts + [jnp.zeros((), jnp.int32)] * (whole.ndim - len(starts))
    return lax.dynamic_update_slice(whole, part, starts)


def place(whole, parts, axis):
    count = len(parts)
    spots = jnp.stack([jnp.asarray(spot, jnp.int32) for _, *pair in parts for spot in pair])
    fresh = isinstance(whole, tuple)
    kind, shape = parts[0][0].dtype, whole if fresh else whole.shape

    def kernel(spots_ref, *refs):
        sources, target, arrived, left = refs[:count], refs[-3 - count], refs[-2], refs[-1]
        buffers = refs[-2 - count : -2]
        loads = [
            pltpu.make_async_copy(sources[at], buffers[at], arrived.at[at]) for at in range(count)
        ]
        stores = []
        for at in range(count):
            spot, half = spots_ref[2 * at], spots_ref[2 * at + 1]
            into = target.at[:, spot, half] if axis == 1 else target.at[spot, :, half]
            stores.append(pltpu.make_async_copy(buffers[at], into, left.at[at]))
        for load in loads:
            load.start()
        for load, store in zip(loads, stores):
            load.wait()
            store.start()
        for store in stores:
            store.wait()

    return pl.pallas_call(
        kernel,
        out_shape=jax.ShapeDtypeStruct(shape, kind),
        grid_spec=pltpu.PrefetchScalarGridSpec(
            num_scalar_prefetch=1,
            grid=(1,),
            in_specs=[pl.BlockSpec(memory_space=pl.ANY)] * (count + (0 if fresh else 1)),
            out_specs=pl.BlockSpec(memory_space=pl.ANY),
            scratch_shapes=[pltpu.VMEM(part.shape, kind) for part, *_ in parts]
            + [pltpu.SemaphoreType.DMA((count,)), pltpu.SemaphoreType.DMA((count,))],
        ),
        input_output_aliases={} if fresh else {1 + count: 0},
        compiler_params=pltpu.CompilerParams(vmem_limit_bytes=40 * 1024 * 1024),
        name="place",
    )(spots, *[part for part, *_ in parts], *([] if fresh else [whole]))


def peek(value):
    ends = [min(size, limit) for size, limit in zip(value.shape[-2:], (8, 128))]
    return lax.slice(value, (0,) * value.ndim, (1,) * (value.ndim - 2) + tuple(ends))


class Pace:
    def __init__(self):
        self.token = None

    def tie(self, value):
        return value if self.token is None else behind(value, self.token)

    def close(self, *values, hold=()):
        hold = [gather for gather in hold if gather.write() is not None]
        held = [gather.buffer for gather in hold]
        taken = len(values) + len(held)

        def kernel(*refs):
            refs[taken][...] = jnp.zeros_like(refs[taken])

        outs = pl.pallas_call(
            kernel,
            out_shape=[jax.ShapeDtypeStruct((8, 128), jnp.float32)]
            + [jax.ShapeDtypeStruct(value.shape, value.dtype) for value in held],
            in_specs=[pl.BlockSpec(memory_space=pl.ANY)] * taken,
            out_specs=[pl.BlockSpec(memory_space=pltpu.VMEM)]
            + [pl.BlockSpec(memory_space=pl.ANY)] * len(held),
            input_output_aliases={len(values) + at: 1 + at for at in range(len(held))},
            name="close",
        )(*values, *held)
        self.token = outs[0]
        for gather, value in zip(hold, outs[1:]):
            gather.buffer = value


class Gather:
    def __init__(self, links, shard):
        self.links, self.piece, self.step, self.level = links, shard, 0, 0
        self.column = blank((links.nz,) + shard.shape, shard.dtype, (shard,))
        self.column = update(self.column, shard[None], [links.z])
        self.found, self.sibling, self.buffer, self.written = None, {}, None, set()

    def along(self, pace, steps=None):
        links, fresh = self.links, []
        self.piece = pace.tie(self.piece)
        while self.step < links.nz - 1 and (steps is None or steps > 0):
            self.step = self.step + 1
            self.piece = links.shift(self.piece, "z")
            self.column = update(self.column, self.piece[None], [(links.z - self.step) % links.nz])
            fresh.append(self.piece)
            steps = None if steps is None else steps - 1
        return fresh

    def wave(self, pace, siblings=True):
        links, fresh = self.links, []
        if self.found is None:
            fresh = self.along(pace)
            self.found = {(0, 0): self.column}
        for key in [key for key in self.found if sum(key) == self.level]:
            self.found[key] = pace.tie(self.found[key])
            if siblings:
                self.sibling[key] = links.swap(self.found[key])
                fresh.append(self.sibling[key])
        self.level = self.level + 1
        for back_a in range(links.na):
            back_b = self.level - back_a
            if 0 <= back_b < links.nb:
                if back_b > 0:
                    value = links.shift(self.found[back_a, back_b - 1], "b")
                else:
                    value = links.shift(self.found[back_a - 1, 0], "a")
                self.found[back_a, back_b] = value
                fresh.append(value)
        return fresh

    def last(self, pace):
        links, fresh = self.links, []
        while self.level < links.na + links.nb - 2:
            fresh = fresh + self.wave(pace)
        for key in self.found:
            if key not in self.sibling:
                self.found[key] = pace.tie(self.found[key])
                self.sibling[key] = links.swap(self.found[key])
                fresh.append(self.sibling[key])
        return fresh

    def write(self):
        links, parts = self.links, []
        nz, rows, width = self.column.shape
        for key in self.sibling:
            if key not in self.written:
                self.written.add(key)
                mine = links.plane(key[0], key[1], links.core)
                theirs = links.plane(key[0], key[1], 1 - links.core)
                parts.append((self.found[key], mine, links.core))
                parts.append((self.sibling[key], theirs, 1 - links.core))
        if parts:
            shape = (nz, links.na * links.nb, 2, rows, width)
            self.buffer = place(shape if self.buffer is None else self.buffer, parts, 1)
        return self.buffer

    def whole(self):
        return self.write().reshape(-1, self.column.shape[2])


class Small:
    def __init__(self, links, row):
        self.links, self.pieces, self.level, self.found = links, [row], 0, None

    def along(self, pace, steps=1):
        while len(self.pieces) < self.links.nz and steps > 0:
            self.pieces.append(self.links.shift(pace.tie(self.pieces[-1]), "z"))
            steps = steps - 1
        return self.pieces[-1:]

    def wave(self, pace):
        links, fresh = self.links, []
        if self.found is None:
            self.along(pace, links.nz)
            self.found = {(0, 0): jnp.stack(self.pieces)}
        for key in [key for key in self.found if sum(key) == self.level]:
            self.found[key] = pace.tie(self.found[key])
        self.level = self.level + 1
        for back_a in range(links.na):
            back_b = self.level - back_a
            if 0 <= back_b < links.nb:
                if back_b > 0:
                    value = links.shift(self.found[back_a, back_b - 1], "b")
                else:
                    value = links.shift(self.found[back_a - 1, 0], "a")
                self.found[back_a, back_b] = value
                fresh.append(value)
        return fresh

    def whole(self, pace):
        links = self.links
        while self.found is None or self.level < links.na + links.nb - 2:
            self.wave(pace)
        parts, places = [], []
        for (back_a, back_b), value in self.found.items():
            parts.append(value)
            plane = links.plane(back_a, back_b, links.core)
            for step in range(links.nz):
                places.append((links.z - step) % links.nz * (links.n1 * links.n2) + plane)
        return place_rows(jnp.concatenate(parts), jnp.stack(places))


def place_rows(found, places):
    count = found.shape[0]
    result = jnp.zeros_like(found)
    spots = jnp.arange(count, dtype=jnp.int32)
    for index in range(count):
        chosen = spots == places[index]
        result = jnp.where(chosen[(slice(None),) + (None,) * (found.ndim - 1)], found[index][None], result)
    return result


def roll_to(value, axis, first):
    size = value.shape[axis]
    if size == 1:
        return value
    doubled = jnp.concatenate([value, value], axis)
    return lax.dynamic_slice_in_dim(doubled, first, size, axis)


def relative_rows(links, left):
    features = left.shape[1]
    nz, n1, n2 = links.sizes
    half = features // (links.count * 2)
    turned = left.T.reshape(nz, n1, n2, 2, half, left.shape[0])
    turned = roll_to(roll_to(roll_to(turned, 0, links.z), 1, links.i1), 2, links.i2)
    turned = roll_to(turned, 3, links.core)
    ordinary = turned.transpose(3, 1, 2, 0, 4, 5)
    if not links.twist:
        return ordinary
    other = turned.transpose(3, 2, 1, 0, 4, 5)
    return jnp.stack(
        [jnp.where(links.core == 0, ordinary[0], other[0]), jnp.where(links.core == 0, other[1], ordinary[1])]
    )


def both_rows(links, left):
    return jnp.concatenate([left[0], links.swap(left[1])], 4)


def halves_total(left, right):
    total = matmul(left.reshape(-1, left.shape[4]), right).astype(jnp.bfloat16)
    return total.reshape(left.shape[:4] + (right.shape[1],))


class Reduce:
    def __init__(self, links, value, kinds):
        self.links, self.value, self.kinds = links, value, list(kinds)
        self.spot, self.moving = value.shape[0] - 1, value[value.shape[0] - 1]

    def step(self, pace, steps=1):
        if not self.kinds:
            return []
        if self.spot == 0:
            self.kinds = self.kinds[1:]
            if not self.kinds:
                return []
            self.value = self.moving
            self.spot, self.moving = self.value.shape[0] - 1, self.value[self.value.shape[0] - 1]
        self.moving = pace.tie(self.moving)
        while self.spot > 0 and steps > 0:
            moved = self.links.shift(self.moving, self.kinds[0])
            self.spot, steps = self.spot - 1, steps - 1
            self.moving = self.value[self.spot].astype(jnp.float32) + moved.astype(jnp.float32)
            if self.spot > 0 or len(self.kinds) > 1:
                self.moving = self.moving.astype(jnp.bfloat16)
        return [self.moving]

    def ring(self, pace):
        return self.step(pace, 1000)

    def done(self, pace):
        while len(self.kinds) > 1 or (self.kinds and self.spot > 0):
            self.ring(pace)
        return self.moving.astype(jnp.float32)


def exchange_along(links, blocks, axis):
    here = (links.z, links.i1, links.i2)[axis]
    size, fresh = links.sizes[axis], blocks
    for steps in range(1, size):
        part = lax.dynamic_slice_in_dim(blocks, (here + steps) % size, 1, axis)
        moved = links.shift(part, axis, steps)
        fresh = lax.dynamic_update_slice_in_dim(fresh, moved, (here - steps) % size, axis)
    return fresh


class Total:
    def __init__(self, links, value):
        self.links, self.value, self.ways = links, value, [None]
        for axis in (2, 1, 0):
            bit = 1
            while bit < links.sizes[axis]:
                self.ways.append((axis, bit))
                bit = bit * 2

    def step(self, pace):
        if self.ways:
            way, self.ways = self.ways[0], self.ways[1:]
            self.value = pace.tie(self.value)
            moved = self.links.swap(self.value) if way is None else self.links.flip(self.value, *way)
            self.value = self.value + moved
        return [self.value]

    def done(self, pace):
        while self.ways:
            self.step(pace)
        return self.value


def all_sum(links, value):
    value = value + links.swap(value)
    for axis in (2, 1, 0):
        bit = 1
        while bit < links.sizes[axis]:
            value = value + links.flip(value, axis, bit)
            bit = bit * 2
    return value


def softmax_parts(scores):
    top_score = jnp.max(scores, -1, keepdims=True)
    powers = jnp.exp(scores - top_score)
    return powers / jnp.sum(powers, -1, keepdims=True)


def attention_backward(query, keys, values, weights, grad_mixed):
    factor = HEAD_DIM ** (-0.5)
    grad_weights = jnp.einsum("qhe,khe->hqk", grad_mixed, values, preferred_element_type=jnp.float32)
    grad_scores = (weights * (grad_weights - jnp.sum(weights * grad_weights, -1, keepdims=True))).astype(jnp.bfloat16)
    grad_values = jnp.einsum(
        "hqk,qhe->khe", weights.astype(jnp.bfloat16), grad_mixed, preferred_element_type=jnp.float32
    )
    grad_query = jnp.einsum("hqk,khe->qhe", grad_scores, keys, preferred_element_type=jnp.float32) * factor
    grad_keys = jnp.einsum("hqk,qhe->khe", grad_scores, query, preferred_element_type=jnp.float32) * factor
    return (grad_query, grad_keys, grad_values)


def total_rows(value):
    return jnp.sum(value.astype(jnp.float32), 0)


def plackett(scores, ranking):
    ordered = scores[ranking]
    count = ordered.shape[0]
    later = jnp.arange(count)[None, :] >= jnp.arange(count)[:, None]
    grid = jnp.where(later, ordered[None, :], MASKED)
    top_score = jnp.max(grid, 1, keepdims=True)
    tails = top_score[:, 0] + jnp.log(jnp.sum(jnp.exp(grid - top_score), 1))
    return jnp.sum(tails - ordered)


def head_pass(state, final, ranking):
    gain_vector, bias_vector, weight = (final[:D], final[D : 2 * D], final[2 * D :])
    normal, scale = standard_deviation(state)
    chosen = lax.reduce_precision(normal * gain_vector + bias_vector, 8, 7)
    scores = jnp.sum(chosen * weight, -1)
    loss, pull = jax.vjp(lambda given: plackett(given, ranking), scores)
    (grad_scores,) = pull(jnp.ones((), jnp.float32))
    grad_chosen = grad_scores[:, None] * weight
    grad_final = jnp.concatenate(
        [
            jnp.sum(grad_chosen * normal, 0),
            jnp.sum(grad_chosen, 0),
            jnp.sum(grad_scores[:, None] * chosen, 0),
        ]
    )
    return (loss, norm_gradient_pass(grad_chosen * gain_vector, normal, scale), grad_final)


def adamw_update(weight, moment, second, average, gradient_value, rate, decay):
    moment_new = BETA_ONE * moment + (1.0 - BETA_ONE) * gradient_value
    second_new = BETA_TWO * second + (1.0 - BETA_TWO) * gradient_value * gradient_value
    moment_hat = moment_new / (1.0 - BETA_ONE**STEP)
    second_hat = second_new / (1.0 - BETA_TWO**STEP)
    weight_new = weight - rate * (moment_hat / (jnp.sqrt(second_hat) + ADAM_EPS) + decay * weight)
    average_new = EMA_KEEP * average + (1.0 - EMA_KEEP) * weight_new
    return (weight_new, moment_new, second_new, average_new)


def low_rows(table, token):
    features, vocabulary = table.shape
    block = 4096

    def kernel(table_ref, token_ref, out_ref):
        out_ref[...] = table_ref[...].T.astype(jnp.bfloat16)

    return pl.pallas_call(
        kernel,
        grid=(pl.cdiv(vocabulary, block),),
        out_shape=jax.ShapeDtypeStruct((vocabulary, features), jnp.bfloat16),
        in_specs=[
            pl.BlockSpec((features, block), lambda at: (0, at)),
            pl.BlockSpec(memory_space=pl.ANY),
        ],
        out_specs=pl.BlockSpec((block, features), lambda at: (at, 0)),
        compiler_params=pltpu.CompilerParams(vmem_limit_bytes=48 * 1024 * 1024),
        name="low_rows",
    )(table, token)


def sum_rows(ids, rows, count):
    tokens, features = rows.shape
    unroll, block = 32, 384

    def kernel(ids_ref, rows_ref, out_ref, squares_ref):
        def clear(at, carry):
            out_ref[pl.ds(at * block, block), :] = jnp.zeros((block, features), jnp.float32)
            return carry

        lax.fori_loop(0, count // block, clear, 0)

        def add(at, carry):
            for step in range(unroll):
                token = at * unroll + step
                spot = ids_ref[token]
                out_ref[pl.ds(spot, 1), :] = out_ref[pl.ds(spot, 1), :] + rows_ref[pl.ds(token, 1), :]
            return carry

        lax.fori_loop(0, tokens // unroll, add, 0)

        def square(at, total):
            value = out_ref[pl.ds(at * block, block), :]
            return total + jnp.sum((value * value).reshape(block // 8, 8, features), 0)

        total = lax.fori_loop(0, count // block, square, jnp.zeros((8, features), jnp.float32))
        squares_ref[0, 0] = jnp.sum(total)

    summed, squares = pl.pallas_call(
        kernel,
        out_shape=(
            jax.ShapeDtypeStruct((count, features), jnp.float32),
            jax.ShapeDtypeStruct((1, 1), jnp.float32),
        ),
        grid_spec=pltpu.PrefetchScalarGridSpec(
            num_scalar_prefetch=1,
            grid=(1,),
            in_specs=[pl.BlockSpec((tokens, features), lambda at, ids: (0, 0))],
            out_specs=[
                pl.BlockSpec((count, features), lambda at, ids: (0, 0), pipeline_mode=pl.Buffered(1)),
                pl.BlockSpec(memory_space=pltpu.SMEM),
            ],
        ),
        compiler_params=pltpu.CompilerParams(vmem_limit_bytes=58 * 1024 * 1024),
        name="sum_rows",
    )(ids, rows)
    return (summed, squares[0, 0])


def table_update(table, moment, second, average, grad_rows, factor):
    features, vocabulary = table.shape
    block = 7296

    def kernel(factor_ref, table_ref, moment_ref, second_ref, average_ref, grad_ref, *outs):
        grad = grad_ref[...].T * factor_ref[0, 0]
        parts = adamw_update(
            table_ref[...], moment_ref[...], second_ref[...], average_ref[...], grad, RATE_MAT, WEIGHT_DECAY
        )
        for out, part in zip(outs, parts):
            out[...] = part

    wide = pl.BlockSpec((features, block), lambda at: (0, at))
    return tuple(
        pl.pallas_call(
            kernel,
            grid=(pl.cdiv(vocabulary, block),),
            out_shape=[jax.ShapeDtypeStruct(table.shape, jnp.float32)] * 4,
            in_specs=[pl.BlockSpec(memory_space=pltpu.SMEM)]
            + [wide] * 4
            + [pl.BlockSpec((block, features), lambda at: (at, 0))],
            out_specs=[wide] * 4,
            compiler_params=pltpu.CompilerParams(vmem_limit_bytes=56 * 1024 * 1024),
            name="table_update",
        )(factor.reshape(1, 1), table, moment, second, average, grad_rows)
    )


def body(
    token_ids,
    seg_lengths,
    rankings,
    table,
    table_m,
    table_v,
    table_ema,
    in_w,
    in_m,
    in_v,
    in_ema,
    out_w,
    out_m,
    out_v,
    out_ema,
    layer_vec,
    vec_m,
    vec_v,
    vec_ema,
    final_vec,
    final_m,
    final_v,
    final_ema,
):
    links = Links()
    core, place, count = links.core, links.dp, links.count
    micro, width = token_ids.shape
    mine_first = core == 0

    pace = Pace()
    low_in, low_out = in_w[0].astype(jnp.bfloat16), out_w[0].astype(jnp.bfloat16)

    def halves(shard):
        rows = shard.shape[0] // 2
        keep = lax.dynamic_slice_in_dim(shard, core * rows, rows, 0)
        give = lax.dynamic_slice_in_dim(shard, (1 - core) * rows, rows, 0)
        got = links.swap(give)
        return (jnp.where(mine_first, keep, got), jnp.where(mine_first, got, keep))

    in_0, in_1 = halves(low_in)
    out_0, out_1 = halves(low_out)
    own_vec, own_final = lax.reduce_precision(layer_vec[0], 8, 7), lax.reduce_precision(final_vec, 8, 7)
    vec_part, final_part = own_vec.shape[0], own_final.shape[0]
    small = Small(links, jnp.concatenate([own_vec, own_final, token_ids.astype(jnp.float32).reshape(-1)]))
    pace.close(in_0, out_0, *small.along(pace))
    w_in_0 = lax.all_gather(in_0, ("dp", "section"), axis=0, tiled=True)
    w_up_1 = lax.all_gather(in_1[:, 3 * D :], ("dp", "section"), axis=0, tiled=True)
    w_out_1 = lax.all_gather(out_1, ("dp", "section"), axis=0, tiled=True)
    out_0, qkv_1 = Gather(links, out_0), Gather(links, in_1[:, : 3 * D])
    pace.close(*small.along(pace))
    table_rows = low_rows(table, pace.token)
    pace.close(*small.along(pace), peek(table_rows))
    pace.close(*small.wave(pace))
    pace.close(*small.wave(pace))
    lengths = lax.dynamic_slice_in_dim(seg_lengths, core, 1, 0)[0]
    small = small.whole(pace)
    small_other = links.swap(small[:, :vec_part])
    own_layer, other_layer = small[:, :vec_part].reshape(-1), small_other.reshape(-1)
    vector_0 = jnp.where(mine_first, own_layer, other_layer)
    vector_1 = jnp.where(mine_first, other_layer, own_layer)
    final = small[:, vec_part : vec_part + final_part].reshape(-1)
    every_ids = small[:, vec_part + final_part :].astype(jnp.int32).reshape(count, micro, width)

    ids_here = lax.dynamic_slice_in_dim(every_ids, core, 1, 1).reshape(-1)
    picked = jnp.take(table_rows, pace.tie(ids_here), axis=0, mode="clip")
    features = picked.shape[1]
    blocks = picked.reshape(links.sizes + (width, features)).transpose(0, 1, 2, 4, 3)
    pace.close(peek(blocks), *out_0.along(pace, 1))
    blocks = exchange_along(links, pace.tie(blocks), 2)
    pace.close(peek(blocks), *out_0.along(pace, 1))
    blocks = exchange_along(links, pace.tie(blocks), 1)
    pace.close(peek(blocks), *out_0.along(pace))
    blocks = exchange_along(links, pace.tie(blocks), 0)
    pace.close(peek(blocks))
    state = blocks.reshape(D, width).T.astype(jnp.float32)

    ranking = lax.dynamic_slice_in_dim(rankings, core, 1, 0)[0]
    position, allowed, last = layout(lengths, width)
    cosine, sine = angles(position)

    first_gain, first_bias, second_gain, second_bias, bias_qkv, bias_attn, bias_up, bias_down = pieces(vector_0)
    normal, scale = standard_deviation(state)
    left = (normal * first_gain + first_bias).astype(jnp.bfloat16)
    right = (normal * second_gain + second_bias).astype(jnp.bfloat16)
    joined = matmul(pace.tie(left), w_in_0[:, : 3 * D]) + bias_qkv
    query = turn(joined[:, :D].reshape(width, HEADS, HEAD_DIM), cosine, sine, 1.0).astype(jnp.bfloat16)
    keys = turn(joined[:, D : 2 * D].reshape(width, HEADS, HEAD_DIM), cosine, sine, 1.0).astype(jnp.bfloat16)
    values = joined[:, 2 * D :].reshape(width, HEADS, HEAD_DIM).astype(jnp.bfloat16)
    weights = softmax_parts(scores_of(query, keys, allowed))
    mixed = (
        jnp.einsum("hqk,khe->qhe", weights.astype(jnp.bfloat16), values, preferred_element_type=jnp.float32)
        .reshape(width, D)
        .astype(jnp.bfloat16)
    )
    pace.close(*out_0.wave(pace), *qkv_1.along(pace, 1), peek(mixed))
    upper = matmul(pace.tie(right), w_in_0[:, 3 * D :]) + bias_up
    active = jax.nn.gelu(upper, approximate=False).astype(jnp.bfloat16)
    pace.close(*out_0.wave(pace), *qkv_1.along(pace, 1), peek(active))
    left_both = both_rows(links, relative_rows(links, left))
    right_both = both_rows(links, relative_rows(links, right))
    pace.close(*out_0.last(pace), *qkv_1.along(pace), peek(left_both), peek(right_both))
    w_out_0 = out_0.whole()
    acts = jnp.concatenate([mixed, active], 1)
    state_1 = (
        state + matmul(mixed, w_out_0[:D]) + bias_attn + (matmul(pace.tie(active), w_out_0[D:]) + bias_down)
    )
    state_1 = lax.reduce_precision(state_1, 8, 7)
    kept = (normal, scale, left, right, upper, query, keys, values, weights, acts)
    pace.close(*qkv_1.wave(pace), peek(state_1))
    pace.close(*qkv_1.wave(pace))
    pace.close(*qkv_1.last(pace))
    w_qkv_1 = qkv_1.whole()
    state_1 = pace.tie(state_1)

    ends = last.shape[0]
    first_gain, first_bias, second_gain, second_bias, bias_qkv, bias_attn, bias_up, bias_down = pieces(vector_1)
    normal, scale = standard_deviation(state_1)
    left = (normal * first_gain + first_bias).astype(jnp.bfloat16)
    pairs = matmul(left, w_qkv_1[:, D:]) + bias_qkv[D:]
    keys = turn(pairs[:, :D].reshape(width, HEADS, HEAD_DIM), cosine, sine, 1.0).astype(jnp.bfloat16)
    values = pairs[:, D:].reshape(width, HEADS, HEAD_DIM).astype(jnp.bfloat16)
    normal_end, scale_end, state_end = normal[last], scale[last], state_1[last]
    cosine_end, sine_end, allowed_end = cosine[last], sine[last], allowed[last]
    left_end = (normal_end * first_gain + first_bias).astype(jnp.bfloat16)
    right_end = (normal_end * second_gain + second_bias).astype(jnp.bfloat16)
    query = matmul(left_end, w_qkv_1[:, :D]) + bias_qkv[:D]
    query = turn(query.reshape(ends, HEADS, HEAD_DIM), cosine_end, sine_end, 1.0).astype(jnp.bfloat16)
    upper = matmul(right_end, w_up_1) + bias_up
    weights = softmax_parts(scores_of(query, keys, allowed_end))
    mixed = (
        jnp.einsum("hqk,khe->qhe", weights.astype(jnp.bfloat16), values, preferred_element_type=jnp.float32)
        .reshape(ends, D)
        .astype(jnp.bfloat16)
    )
    active = jax.nn.gelu(upper, approximate=False).astype(jnp.bfloat16)
    branch = matmul(mixed, w_out_1[:D]) + bias_attn + (matmul(active, w_out_1[D:]) + bias_down)
    loss, grad_end, grad_final = head_pass(state_end + branch, final, ranking)

    low_end = grad_end.astype(jnp.bfloat16)
    grad_mixed = dot_cols(low_end, w_out_1[:D]).astype(jnp.bfloat16).reshape(ends, HEADS, HEAD_DIM)
    grad_upper = (dot_cols(low_end, w_out_1[D:]) * gelu_slope(upper)).astype(jnp.bfloat16)
    grad_query, grad_keys, grad_values = attention_backward(query, keys, values, weights, grad_mixed)
    grad_query = turn(grad_query, cosine_end, sine_end, -1.0).reshape(ends, D).astype(jnp.bfloat16)
    grad_pairs = jnp.concatenate(
        [turn(grad_keys, cosine, sine, -1.0).reshape(width, D), grad_values.reshape(width, D)], 1
    ).astype(jnp.bfloat16)
    back_left = dot_cols(grad_pairs, w_qkv_1[:, D:])
    back_left_end = dot_cols(grad_query, w_qkv_1[:, :D])
    back_right_end = dot_cols(grad_upper, w_up_1)
    sum_end = total_rows(low_end)
    sum_vec_1 = jnp.concatenate(
        [
            jnp.sum(back_left * normal, 0) + jnp.sum(back_left_end * normal_end, 0),
            jnp.sum(back_left, 0) + jnp.sum(back_left_end, 0),
            jnp.sum(back_right_end * normal_end, 0),
            jnp.sum(back_right_end, 0),
            total_rows(grad_query),
            total_rows(grad_pairs),
            sum_end,
            total_rows(grad_upper),
            sum_end,
        ]
    )
    row_index = jnp.arange(width, dtype=jnp.int32)
    extra = back_left_end * first_gain + back_right_end * second_gain
    pulled = back_left * first_gain
    landed = jnp.zeros_like(pulled)
    for end in range(ends):
        here = (row_index == last[end])[:, None]
        pulled = pulled + jnp.where(here, extra[end][None], 0.0)
        landed = landed + jnp.where(here, grad_end[end][None], 0.0)
    grad_state = landed + norm_gradient_pass(pulled, normal, scale)
    grad_state = lax.reduce_precision(grad_state, 8, 7).astype(jnp.bfloat16)

    pairs_both = both_rows(links, relative_rows(links, left))
    pairs_grad = jnp.concatenate([grad_pairs, links.swap(grad_pairs)])
    factors = jnp.concatenate([left_end, right_end, mixed, active, grad_query, grad_upper, low_end], 1)
    every_factor = lax.all_gather(factors, ("dp", "section"), axis=0, tiled=True)
    in_rows, out_rows = in_w.shape[1], out_w.shape[1]

    normal, scale, left, right, upper, query, keys, values, weights, acts = kept
    first_gain, first_bias, second_gain, second_bias = pieces(vector_0)[:4]
    low_state = grad_state
    pair_sum = Reduce(links, halves_total(pairs_both, pairs_grad), "baz")
    pace.close(peek(pair_sum.moving), peek(low_state))
    low_state = pace.tie(low_state)
    out_half = dot_rows(acts, low_state).astype(jnp.bfloat16)
    out_half = lax.psum_scatter(out_half, ("dp", "section"), scatter_dimension=0, tiled=True)
    grad_mixed = dot_cols(low_state, w_out_0[:D]).astype(jnp.bfloat16).reshape(width, HEADS, HEAD_DIM)
    grad_upper = (dot_cols(low_state, w_out_0[D:]) * gelu_slope(upper)).astype(jnp.bfloat16)
    upper_both = jnp.concatenate([grad_upper, links.swap(grad_upper)])
    pace.close(*map(peek, pair_sum.ring(pace)), peek(grad_mixed), peek(upper_both))
    up_sum = halves_total(right_both, pace.tie(upper_both))
    grad_query, grad_keys, grad_values = attention_backward(query, keys, values, weights, pace.tie(grad_mixed))
    grad_joined = jnp.concatenate(
        [
            turn(grad_query, cosine, sine, -1.0).reshape(width, D),
            turn(grad_keys, cosine, sine, -1.0).reshape(width, D),
            grad_values.reshape(width, D),
        ],
        1,
    ).astype(jnp.bfloat16)
    pace.close(*map(peek, pair_sum.ring(pace)), peek(up_sum), peek(grad_joined))
    grad_joined = pace.tie(grad_joined)
    back_left = dot_cols(grad_joined, w_in_0[:, : 3 * D])
    back_right = dot_cols(grad_upper, w_in_0[:, 3 * D :])
    grad_embedded = low_state.astype(jnp.float32) + norm_gradient_pass(
        back_left * first_gain + back_right * second_gain, normal, scale
    )
    joined_both = jnp.concatenate([grad_joined, links.swap(grad_joined)])
    blocks = grad_embedded.astype(jnp.bfloat16).T.reshape(links.sizes + (features, width))
    pace.close(*map(peek, pair_sum.step(pace)), peek(joined_both), peek(blocks))
    blocks = exchange_along(links, pace.tie(blocks), 2)
    qkv_sum = halves_total(left_both, pace.tie(joined_both))
    pace.close(*map(peek, pair_sum.step(pace)), peek(blocks), peek(qkv_sum))
    rest_sum = Reduce(links, jnp.concatenate([qkv_sum, up_sum], 4), "baz")
    blocks = exchange_along(links, pace.tie(blocks), 1)
    back_left, back_right = pace.tie(back_left), pace.tie(back_right)
    sum_state = total_rows(low_state)
    sum_vec_0 = jnp.concatenate(
        [
            jnp.sum(back_left * normal, 0),
            jnp.sum(back_left, 0),
            jnp.sum(back_right * normal, 0),
            jnp.sum(back_right, 0),
            total_rows(grad_joined),
            sum_state,
            total_rows(grad_upper),
            sum_state,
        ]
    )
    packed = jnp.concatenate([sum_vec_0, sum_vec_1, grad_final, loss[None], jnp.zeros((127,), jnp.float32)])
    packed = Total(links, packed.reshape(-1, 128))
    pace.close(*map(peek, pair_sum.step(pace)), peek(blocks), packed.value)
    blocks = exchange_along(links, pace.tie(blocks), 0)
    pace.close(peek(blocks), *packed.step(pace))
    blocks = pace.tie(blocks)
    spread_mine = blocks.reshape(count, features, width).transpose(0, 2, 1)
    spread_other = links.swap(spread_mine)
    spread = jnp.stack(
        [jnp.where(mine_first, spread_mine, spread_other), jnp.where(mine_first, spread_other, spread_mine)], 1
    ).reshape(count * micro * width, features)
    table_grad, table_squares = sum_rows(every_ids.reshape(-1), spread.astype(jnp.float32), table.shape[1])
    pace.close(*map(peek, rest_sum.ring(pace)), peek(table_grad))
    pace.close(*map(peek, rest_sum.ring(pace)))
    pace.close(*map(peek, rest_sum.step(pace)), *packed.step(pace))
    pace.close(*map(peek, rest_sum.step(pace)), *packed.step(pace))
    pace.close(*map(peek, rest_sum.ring(pace)), *packed.step(pace))
    in_half, pair_half = rest_sum.done(pace), pair_sum.done(pace)

    def factor_part(begin, size):
        return every_factor[:, begin : begin + size]

    left_own = lax.dynamic_slice_in_dim(factor_part(0, D), place * in_rows, in_rows, 1)
    right_own = lax.dynamic_slice_in_dim(factor_part(D, D), place * in_rows, in_rows, 1)
    acts_own = lax.dynamic_slice_in_dim(factor_part(2 * D, D + FF), place * out_rows, out_rows, 1)
    query_part = factor_part(3 * D + FF, D)
    upper_part = factor_part(4 * D + FF, FF)
    end_part = factor_part(4 * D + 2 * FF, D)
    grad_in_query = dot_rows(left_own, query_part)
    grad_in_upper = dot_rows(right_own, upper_part)
    grad_out_1 = dot_rows(acts_own, end_part)


    packed = packed.done(pace).reshape(-1)
    vec_size = sum_vec_0.shape[0]
    shard_vec = lax.dynamic_slice_in_dim(packed, core * vec_size + place * vec_part, vec_part, 0)
    shard_fin = lax.dynamic_slice_in_dim(packed, 2 * vec_size + place * final_part, final_part, 0)
    loss_sum = packed[2 * vec_size + 3 * D]

    in_other, out_other, pair_other = links.swap(in_half), links.swap(out_half), links.swap(pair_half)
    grad_in_0 = jnp.concatenate([in_half, in_other], 0)
    out_half = out_half.astype(jnp.float32)
    grad_out_0 = jnp.concatenate([out_half, out_other.astype(jnp.float32)], 0)
    grad_in_1 = jnp.concatenate(
        [grad_in_query, jnp.concatenate([pair_other, pair_half], 0), grad_in_upper], 1
    )
    shard_in = jnp.where(mine_first, grad_in_0, grad_in_1)
    shard_out = jnp.where(mine_first, grad_out_0, grad_out_1)

    squares = (
        jnp.sum(shard_in * shard_in)
        + jnp.sum(shard_out * shard_out)
        + jnp.sum(shard_vec * shard_vec)
        + jnp.where(mine_first, table_squares + jnp.sum(shard_fin * shard_fin), 0.0)
    )
    total_squares = all_sum(links, jnp.broadcast_to(squares, (8, 128)))[0, 0]
    grad_norm = jnp.sqrt(total_squares)
    factor = jnp.minimum(1.0, CLIP_NORM / (grad_norm + 1e-06))
    table_parts = table_update(table, table_m, table_v, table_ema, table_grad, factor)
    in_parts = adamw_update(
        in_w, in_m, in_v, in_ema, shard_in.reshape(in_w.shape) * factor, RATE_MAT, WEIGHT_DECAY
    )
    out_parts = adamw_update(
        out_w, out_m, out_v, out_ema, shard_out.reshape(out_w.shape) * factor, RATE_MAT, WEIGHT_DECAY
    )
    vec_parts = adamw_update(
        layer_vec, vec_m, vec_v, vec_ema, shard_vec.reshape(layer_vec.shape) * factor, RATE_VEC, 0.0
    )
    final_parts = adamw_update(final_vec, final_m, final_v, final_ema, shard_fin * factor, RATE_VEC, 0.0)
    return (loss_sum, grad_norm) + table_parts + in_parts + out_parts + vec_parts + final_parts


def solution(mesh):
    in_specs = (
        P("dp", None),
        P("dp", None),
        P("dp", None),
        P("dp", None),
        P("dp", None),
        P("dp", None),
        P("dp", None),
        P("section", "dp", None),
        P("section", "dp", None),
        P("section", "dp", None),
        P("section", "dp", None),
        P("section", "dp", None),
        P("section", "dp", None),
        P("section", "dp", None),
        P("section", "dp", None),
        P("section", "dp"),
        P("section", "dp"),
        P("section", "dp"),
        P("section", "dp"),
        P("dp"),
        P("dp"),
        P("dp"),
        P("dp"),
    )
    out_specs = (
        P(),
        P(),
        P("dp", None),
        P("dp", None),
        P("dp", None),
        P("dp", None),
        P("section", "dp", None),
        P("section", "dp", None),
        P("section", "dp", None),
        P("section", "dp", None),
        P("section", "dp", None),
        P("section", "dp", None),
        P("section", "dp", None),
        P("section", "dp", None),
        P("section", "dp"),
        P("section", "dp"),
        P("section", "dp"),
        P("section", "dp"),
        P("dp"),
        P("dp"),
        P("dp"),
        P("dp"),
    )
    return jax.shard_map(body, mesh=mesh, in_specs=in_specs, out_specs=out_specs, check_vma=False)
```

```python
import jax
import jax.numpy as jnp
from jax import lax
from jax.experimental import pallas as pl
from jax.experimental.pallas import tpu as pltpu
from jax.sharding import PartitionSpec as P

D = 1024
HEADS = 16
HEAD_DIM = 64
FF = 4096
ROT = 16
STEP = 10


EPS_NORM = 1e-05
CLIP_NORM = 0.05
BETA_ONE = 0.9
BETA_TWO = 0.95
ADAM_EPS = 1e-08
RATE_MAT = 0.1
RATE_VEC = 0.3
WEIGHT_DECAY = 0.1
EMA_KEEP = 0.75
MASKED = -1e30


def matmul(left_operand, right_operand):
    return jnp.dot(left_operand, right_operand, preferred_element_type=jnp.float32)


def dot_rows(left_operand, right_operand):
    return lax.dot_general(
        left_operand, right_operand, (((0,), (0,)), ((), ())), preferred_element_type=jnp.float32
    )


def dot_cols(left_operand, right_operand):
    return lax.dot_general(
        left_operand, right_operand, (((1,), (1,)), ((), ())), preferred_element_type=jnp.float32
    )


def standard_deviation(value_rows):
    center = value_rows - jnp.mean(value_rows, -1, keepdims=True)
    scale_factor = lax.rsqrt(jnp.mean(center * center, -1, keepdims=True) + EPS_NORM)
    return (center * scale_factor, scale_factor)


def norm_gradient_pass(gradient_normalized, input_normalized, scale_factor):
    return scale_factor * (
        gradient_normalized
        - jnp.mean(gradient_normalized, -1, keepdims=True)
        - input_normalized * jnp.mean(gradient_normalized * input_normalized, -1, keepdims=True)
    )


def layout(lengths, width):
    bounds = jnp.cumsum(lengths)
    starts = bounds - lengths
    places = jnp.arange(width, dtype=jnp.int32)
    segment = jnp.sum((places[:, None] >= bounds[None, :]).astype(jnp.int32), 1)
    pieces_count = lengths.shape[0]
    owner = jnp.minimum(segment, pieces_count - 1)
    chosen = jnp.arange(pieces_count, dtype=jnp.int32)[None, :] == owner[:, None]
    begin = jnp.sum(jnp.where(chosen, starts[None, :], 0), 1)
    position = places - begin + jnp.where(segment > 0, lengths[0], 0)
    same = (segment[:, None] == segment[None, :]) & (places[None, :] <= places[:, None])
    prompt = (segment[None, :] == 0) & (segment[:, None] > 0) & (segment[:, None] < pieces_count)
    return (position, same | prompt, bounds[1:] - 1)


def angles(position):
    half = ROT // 2
    freqs = 10000.0 ** (-2.0 * jnp.arange(half, dtype=jnp.float32) / ROT)
    phase = position.astype(jnp.float32)[:, None] * freqs[None, :]
    return (jnp.cos(phase)[:, None, :], jnp.sin(phase)[:, None, :])


def turn(value_rows, cosine, sine, sign):
    half = cosine.shape[-1]
    first = value_rows[..., :half]
    second = value_rows[..., half : 2 * half]
    return jnp.concatenate(
        [
            first * cosine - sign * second * sine,
            second * cosine + sign * first * sine,
            value_rows[..., 2 * half :],
        ],
        -1,
    )


def pieces(vector):
    amounts = [D, D, D, D, 3 * D, D, FF, D]
    parts = []
    offset = 0
    for amount in amounts:
        parts.append(vector[offset : offset + amount])
        offset = offset + amount
    return parts


def gelu_slope(value_rows):
    cumulative = 0.5 * (1.0 + jax.scipy.special.erf(value_rows * 0.7071067811865476))
    return cumulative + value_rows * jnp.exp(-0.5 * value_rows * value_rows) * 0.3989422804014327


def scores_of(query_rows, key_rows, allowed):
    raw = jnp.einsum(
        "qhe,khe->hqk", query_rows, key_rows, preferred_element_type=jnp.float32
    ) * HEAD_DIM ** (-0.5)
    return jnp.where(allowed[None], raw, MASKED)


def grid(count):
    return {16: (4, 2, 2), 128: (8, 4, 4)}.get(count, (count, 1, 1))


class Links:
    def __init__(self):
        self.count = lax.axis_size("dp")
        self.sizes = grid(self.count)
        self.nz, self.n1, self.n2 = self.sizes
        self.core = lax.axis_index("section")
        self.dp = lax.axis_index("dp")
        self.z = self.dp // (self.n1 * self.n2)
        self.i1 = self.dp // self.n2 % self.n1
        self.i2 = self.dp % self.n2
        self.twist = self.n1 == self.n2
        self.na, self.nb = self.n2, self.n1

    def axis_of(self, kind, core):
        if kind == "z":
            return 0
        if kind == "a":
            return 1 if core == 1 and self.twist else 2
        if kind == "b":
            return 2 if core == 1 and self.twist else 1
        return kind

    def pairs(self, kind, target):
        result = []
        for core in range(2):
            axis = self.axis_of(kind, core)
            for place in range(self.count):
                spot = [place // (self.n1 * self.n2), place // self.n2 % self.n1, place % self.n2]
                spot[axis] = target(spot[axis], self.sizes[axis])
                to = (spot[0] * self.n1 + spot[1]) * self.n2 + spot[2]
                result.append((core * self.count + place, core * self.count + to))
        return result

    def shift(self, value, kind, steps=1):
        pairs = self.pairs(kind, lambda place, size: (place + steps) % size)
        return lax.ppermute(value, ("section", "dp"), pairs)

    def flip(self, value, kind, bit):
        return lax.ppermute(value, ("section", "dp"), self.pairs(kind, lambda place, size: place ^ bit))

    def swap(self, value):
        return lax.ppermute(value, "section", [(0, 1), (1, 0)])

    def plane(self, back_a, back_b, core):
        first = (self.i1 - back_b) % self.n1
        second = (self.i2 - back_a) % self.n2
        usual = first * self.n2 + second
        if not self.twist:
            return usual
        other = (self.i1 - back_a) % self.n1 * self.n2 + (self.i2 - back_b) % self.n2
        return jnp.where(core == 0, usual, other)


def nothing(*refs):
    pass


def blank(shape, kind, after):
    return pl.pallas_call(
        nothing,
        out_shape=jax.ShapeDtypeStruct(shape, kind),
        in_specs=[pl.BlockSpec(memory_space=pl.ANY)] * len(after),
        out_specs=pl.BlockSpec(memory_space=pl.ANY),
        name="blank",
    )(*after)


def behind(value, *after):
    return pl.pallas_call(
        nothing,
        out_shape=jax.ShapeDtypeStruct(value.shape, value.dtype),
        in_specs=[pl.BlockSpec(memory_space=pl.ANY)] * (1 + len(after)),
        out_specs=pl.BlockSpec(memory_space=pl.ANY),
        input_output_aliases={0: 0},
        name="behind",
    )(value, *after)


def update(whole, part, starts):
    starts = [jnp.asarray(start, jnp.int32) for start in starts]
    starts = starts + [jnp.zeros((), jnp.int32)] * (whole.ndim - len(starts))
    return lax.dynamic_update_slice(whole, part, starts)


def place(whole, parts, axis):
    count = len(parts)
    spots = jnp.stack([jnp.asarray(spot, jnp.int32) for _, *pair in parts for spot in pair])
    fresh = isinstance(whole, tuple)
    kind, shape = parts[0][0].dtype, whole if fresh else whole.shape

    def kernel(spots_ref, *refs):
        sources, target, arrived, left = refs[:count], refs[-3 - count], refs[-2], refs[-1]
        buffers = refs[-2 - count : -2]
        loads = [
            pltpu.make_async_copy(sources[at], buffers[at], arrived.at[at]) for at in range(count)
        ]
        stores = []
        for at in range(count):
            spot, half = spots_ref[2 * at], spots_ref[2 * at + 1]
            into = target.at[:, spot, half] if axis == 1 else target.at[spot, :, half]
            stores.append(pltpu.make_async_copy(buffers[at], into, left.at[at]))
        for load in loads:
            load.start()
        for load, store in zip(loads, stores):
            load.wait()
            store.start()
        for store in stores:
            store.wait()

    return pl.pallas_call(
        kernel,
        out_shape=jax.ShapeDtypeStruct(shape, kind),
        grid_spec=pltpu.PrefetchScalarGridSpec(
            num_scalar_prefetch=1,
            grid=(1,),
            in_specs=[pl.BlockSpec(memory_space=pl.ANY)] * (count + (0 if fresh else 1)),
            out_specs=pl.BlockSpec(memory_space=pl.ANY),
            scratch_shapes=[pltpu.VMEM(part.shape, kind) for part, *_ in parts]
            + [pltpu.SemaphoreType.DMA((count,)), pltpu.SemaphoreType.DMA((count,))],
        ),
        input_output_aliases={} if fresh else {1 + count: 0},
        compiler_params=pltpu.CompilerParams(vmem_limit_bytes=40 * 1024 * 1024),
        name="place",
    )(spots, *[part for part, *_ in parts], *([] if fresh else [whole]))


def peek(value):
    ends = [min(size, limit) for size, limit in zip(value.shape[-2:], (8, 128))]
    return lax.slice(value, (0,) * value.ndim, (1,) * (value.ndim - 2) + tuple(ends))


class Pace:
    def __init__(self):
        self.token = None

    def tie(self, value):
        return value if self.token is None else behind(value, self.token)

    def close(self, *values, hold=()):
        hold = [gather for gather in hold if gather.write() is not None]
        held = [gather.buffer for gather in hold]
        taken = len(values) + len(held)

        def kernel(*refs):
            refs[taken][...] = jnp.zeros_like(refs[taken])

        outs = pl.pallas_call(
            kernel,
            out_shape=[jax.ShapeDtypeStruct((8, 128), jnp.float32)]
            + [jax.ShapeDtypeStruct(value.shape, value.dtype) for value in held],
            in_specs=[pl.BlockSpec(memory_space=pl.ANY)] * taken,
            out_specs=[pl.BlockSpec(memory_space=pltpu.VMEM)]
            + [pl.BlockSpec(memory_space=pl.ANY)] * len(held),
            input_output_aliases={len(values) + at: 1 + at for at in range(len(held))},
            name="close",
        )(*values, *held)
        self.token = outs[0]
        for gather, value in zip(hold, outs[1:]):
            gather.buffer = value


class Gather:
    def __init__(self, links, shard):
        self.links, self.piece, self.step, self.level = links, shard, 0, 0
        self.column = blank((links.nz,) + shard.shape, shard.dtype, (shard,))
        self.column = update(self.column, shard[None], [links.z])
        self.found, self.sibling, self.buffer, self.written = None, {}, None, set()

    def along(self, pace, steps=None):
        links, fresh = self.links, []
        self.piece = pace.tie(self.piece)
        while self.step < links.nz - 1 and (steps is None or steps > 0):
            self.step = self.step + 1
            self.piece = links.shift(self.piece, "z")
            self.column = update(self.column, self.piece[None], [(links.z - self.step) % links.nz])
            fresh.append(self.piece)
            steps = None if steps is None else steps - 1
        return fresh

    def wave(self, pace, siblings=True):
        links, fresh = self.links, []
        if self.found is None:
            fresh = self.along(pace)
            self.found = {(0, 0): self.column}
        for key in [key for key in self.found if sum(key) == self.level]:
            self.found[key] = pace.tie(self.found[key])
            if siblings:
                self.sibling[key] = links.swap(self.found[key])
                fresh.append(self.sibling[key])
        self.level = self.level + 1
        for back_a in range(links.na):
            back_b = self.level - back_a
            if 0 <= back_b < links.nb:
                if back_b > 0:
                    value = links.shift(self.found[back_a, back_b - 1], "b")
                else:
                    value = links.shift(self.found[back_a - 1, 0], "a")
                self.found[back_a, back_b] = value
                fresh.append(value)
        return fresh

    def last(self, pace):
        links, fresh = self.links, []
        while self.level < links.na + links.nb - 2:
            fresh = fresh + self.wave(pace)
        for key in self.found:
            if key not in self.sibling:
                self.found[key] = pace.tie(self.found[key])
                self.sibling[key] = links.swap(self.found[key])
                fresh.append(self.sibling[key])
        return fresh

    def write(self):
        links, parts = self.links, []
        nz, rows, width = self.column.shape
        for key in self.sibling:
            if key not in self.written:
                self.written.add(key)
                mine = links.plane(key[0], key[1], links.core)
                theirs = links.plane(key[0], key[1], 1 - links.core)
                parts.append((self.found[key], mine, links.core))
                parts.append((self.sibling[key], theirs, 1 - links.core))
        if parts:
            shape = (nz, links.na * links.nb, 2, rows, width)
            self.buffer = place(shape if self.buffer is None else self.buffer, parts, 1)
        return self.buffer

    def whole(self):
        return self.write().reshape(-1, self.column.shape[2])


class Small:
    def __init__(self, links, row):
        self.links, self.pieces, self.level, self.found = links, [row], 0, None

    def along(self, pace, steps=1):
        while len(self.pieces) < self.links.nz and steps > 0:
            self.pieces.append(self.links.shift(pace.tie(self.pieces[-1]), "z"))
            steps = steps - 1
        return self.pieces[-1:]

    def wave(self, pace):
        links, fresh = self.links, []
        if self.found is None:
            self.along(pace, links.nz)
            self.found = {(0, 0): jnp.stack(self.pieces)}
        for key in [key for key in self.found if sum(key) == self.level]:
            self.found[key] = pace.tie(self.found[key])
        self.level = self.level + 1
        for back_a in range(links.na):
            back_b = self.level - back_a
            if 0 <= back_b < links.nb:
                if back_b > 0:
                    value = links.shift(self.found[back_a, back_b - 1], "b")
                else:
                    value = links.shift(self.found[back_a - 1, 0], "a")
                self.found[back_a, back_b] = value
                fresh.append(value)
        return fresh

    def whole(self, pace):
        links = self.links
        while self.found is None or self.level < links.na + links.nb - 2:
            self.wave(pace)
        parts, places = [], []
        for (back_a, back_b), value in self.found.items():
            parts.append(value)
            plane = links.plane(back_a, back_b, links.core)
            for step in range(links.nz):
                places.append((links.z - step) % links.nz * (links.n1 * links.n2) + plane)
        return place_rows(jnp.concatenate(parts), jnp.stack(places))


def place_rows(found, places):
    count = found.shape[0]
    result = jnp.zeros_like(found)
    spots = jnp.arange(count, dtype=jnp.int32)
    for index in range(count):
        chosen = spots == places[index]
        result = jnp.where(chosen[(slice(None),) + (None,) * (found.ndim - 1)], found[index][None], result)
    return result


def roll_to(value, axis, first):
    size = value.shape[axis]
    if size == 1:
        return value
    doubled = jnp.concatenate([value, value], axis)
    return lax.dynamic_slice_in_dim(doubled, first, size, axis)


def relative_rows(links, left):
    features = left.shape[1]
    nz, n1, n2 = links.sizes
    half = features // (links.count * 2)
    turned = left.T.reshape(nz, n1, n2, 2, half, left.shape[0])
    turned = roll_to(roll_to(roll_to(turned, 0, links.z), 1, links.i1), 2, links.i2)
    turned = roll_to(turned, 3, links.core)
    ordinary = turned.transpose(3, 1, 2, 0, 4, 5)
    if not links.twist:
        return ordinary
    other = turned.transpose(3, 2, 1, 0, 4, 5)
    return jnp.stack(
        [jnp.where(links.core == 0, ordinary[0], other[0]), jnp.where(links.core == 0, other[1], ordinary[1])]
    )


def both_rows(links, left):
    return jnp.concatenate([left[0], links.swap(left[1])], 4)


def halves_total(left, right):
    total = matmul(left.reshape(-1, left.shape[4]), right).astype(jnp.bfloat16)
    return total.reshape(left.shape[:4] + (right.shape[1],))


class Reduce:
    def __init__(self, links, value, kinds):
        self.links, self.value, self.kinds = links, value, list(kinds)
        self.spot, self.moving = value.shape[0] - 1, value[value.shape[0] - 1]

    def step(self, pace, steps=1):
        if not self.kinds:
            return []
        if self.spot == 0:
            self.kinds = self.kinds[1:]
            if not self.kinds:
                return []
            self.value = self.moving
            self.spot, self.moving = self.value.shape[0] - 1, self.value[self.value.shape[0] - 1]
        self.moving = pace.tie(self.moving)
        while self.spot > 0 and steps > 0:
            moved = self.links.shift(self.moving, self.kinds[0])
            self.spot, steps = self.spot - 1, steps - 1
            self.moving = self.value[self.spot].astype(jnp.float32) + moved.astype(jnp.float32)
            if self.spot > 0 or len(self.kinds) > 1:
                self.moving = self.moving.astype(jnp.bfloat16)
        return [self.moving]

    def ring(self, pace):
        return self.step(pace, 1000)

    def done(self, pace):
        while len(self.kinds) > 1 or (self.kinds and self.spot > 0):
            self.ring(pace)
        return self.moving.astype(jnp.float32)


def exchange_along(links, blocks, axis):
    here = (links.z, links.i1, links.i2)[axis]
    size, fresh = links.sizes[axis], blocks
    for steps in range(1, size):
        part = lax.dynamic_slice_in_dim(blocks, (here + steps) % size, 1, axis)
        moved = links.shift(part, axis, steps)
        fresh = lax.dynamic_update_slice_in_dim(fresh, moved, (here - steps) % size, axis)
    return fresh


class Total:
    def __init__(self, links, value):
        self.links, self.value, self.ways = links, value, [None]
        for axis in (2, 1, 0):
            bit = 1
            while bit < links.sizes[axis]:
                self.ways.append((axis, bit))
                bit = bit * 2

    def step(self, pace):
        if self.ways:
            way, self.ways = self.ways[0], self.ways[1:]
            self.value = pace.tie(self.value)
            moved = self.links.swap(self.value) if way is None else self.links.flip(self.value, *way)
            self.value = self.value + moved
        return [self.value]

    def done(self, pace):
        while self.ways:
            self.step(pace)
        return self.value


def all_sum(links, value):
    value = value + links.swap(value)
    for axis in (2, 1, 0):
        bit = 1
        while bit < links.sizes[axis]:
            value = value + links.flip(value, axis, bit)
            bit = bit * 2
    return value


def softmax_parts(scores):
    top_score = jnp.max(scores, -1, keepdims=True)
    powers = jnp.exp(scores - top_score)
    return powers / jnp.sum(powers, -1, keepdims=True)


def spin_tables(cosine, sine):
    rows, _, half = cosine.shape
    cosine, sine = cosine[:, 0], sine[:, 0]
    rest = HEAD_DIM - 2 * half
    none = jnp.zeros((rows, half), jnp.float32)
    own = jnp.concatenate([cosine, cosine, jnp.ones((rows, rest), jnp.float32)], 1)
    above = jnp.concatenate([-sine, none, jnp.zeros((rows, rest), jnp.float32)], 1)
    below = jnp.concatenate([none, sine, jnp.zeros((rows, rest), jnp.float32)], 1)
    return tuple(jnp.concatenate([part, part], 1) for part in (own, above, below))


def spin(value, own, above, below, sign):
    half, lanes = ROT // 2, 2 * HEAD_DIM
    turned = pltpu.roll(value, lanes - half, 1) * above + pltpu.roll(value, half, 1) * below
    return value * own + sign * turned


def head_weights(query, keys, seen):
    scores = jnp.where(seen, dot_cols(query, keys) * HEAD_DIM ** (-0.5), MASKED)
    powers = jnp.exp(scores - jnp.max(scores, -1, keepdims=True))
    return powers / jnp.sum(powers, -1, keepdims=True)


def attend(joined, tables, allowed):
    rows, lanes = joined.shape[0], 2 * HEAD_DIM

    def kernel(joined_ref, own_ref, above_ref, below_ref, seen_ref, query_ref, keys_ref, values_ref, mixed_ref):
        own, above, below = own_ref[...], above_ref[...], below_ref[...]
        seen = seen_ref[...] > 0.5
        lower = lax.broadcasted_iota(jnp.int32, (rows, lanes), 1) < HEAD_DIM
        for pair in range(D // lanes):
            at = slice(pair * lanes, (pair + 1) * lanes)
            query = spin(joined_ref[:, pair * lanes : (pair + 1) * lanes], own, above, below, 1.0)
            keys = spin(joined_ref[:, D + pair * lanes : D + (pair + 1) * lanes], own, above, below, 1.0)
            keys = keys.astype(jnp.bfloat16)
            values = joined_ref[:, 2 * D + pair * lanes : 2 * D + (pair + 1) * lanes].astype(jnp.bfloat16)
            query_ref[:, at], keys_ref[:, at], values_ref[:, at] = query.astype(jnp.bfloat16), keys, values
            parts = []
            for head in range(2):
                mine = lower if head == 0 else jnp.logical_not(lower)
                weights = head_weights(jnp.where(mine, query, 0.0).astype(jnp.bfloat16), keys, seen)
                parts.append(matmul(weights.astype(jnp.bfloat16), values))
            mixed_ref[:, at] = jnp.where(lower, parts[0], parts[1]).astype(jnp.bfloat16)

    return pl.pallas_call(
        kernel,
        out_shape=[jax.ShapeDtypeStruct((rows, D), jnp.bfloat16)] * 4,
        compiler_params=pltpu.CompilerParams(vmem_limit_bytes=40 * 1024 * 1024),
        name="attend",
    )(joined, *tables, allowed)


def attend_back(query, keys, values, grad_mixed, tables, allowed):
    rows, lanes = query.shape[0], 2 * HEAD_DIM

    def kernel(
        query_ref, keys_ref, values_ref, grad_ref, own_ref, above_ref, below_ref, seen_ref, joined_ref
    ):
        own, above, below = own_ref[...], above_ref[...], below_ref[...]
        seen = seen_ref[...] > 0.5
        lower = lax.broadcasted_iota(jnp.int32, (rows, lanes), 1) < HEAD_DIM
        factor = HEAD_DIM ** (-0.5)
        for pair in range(D // lanes):
            at = slice(pair * lanes, (pair + 1) * lanes)
            query, keys, values, grad = query_ref[:, at], keys_ref[:, at], values_ref[:, at], grad_ref[:, at]
            wide_query, wide_grad = query.astype(jnp.float32), grad.astype(jnp.float32)
            parts = []
            for head in range(2):
                mine = lower if head == 0 else jnp.logical_not(lower)
                weights = head_weights(jnp.where(mine, wide_query, 0.0).astype(jnp.bfloat16), keys, seen)
                pulled = dot_cols(jnp.where(mine, wide_grad, 0.0).astype(jnp.bfloat16), values)
                pulled = weights * (pulled - jnp.sum(weights * pulled, -1, keepdims=True))
                pulled = pulled.astype(jnp.bfloat16)
                parts.append(
                    (
                        matmul(pulled, keys) * factor,
                        dot_rows(pulled, query) * factor,
                        dot_rows(weights.astype(jnp.bfloat16), grad),
                    )
                )
            grads = [jnp.where(lower, first, second) for first, second in zip(*parts)]
            for third in range(2):
                grads[third] = spin(grads[third], own, above, below, -1.0)
            for third in range(3):
                start = third * D + pair * lanes
                joined_ref[:, start : start + lanes] = grads[third].astype(jnp.bfloat16)

    return pl.pallas_call(
        kernel,
        out_shape=jax.ShapeDtypeStruct((rows, 3 * D), jnp.bfloat16),
        compiler_params=pltpu.CompilerParams(vmem_limit_bytes=40 * 1024 * 1024),
        name="attend_back",
    )(query, keys, values, grad_mixed, *tables, allowed)


def attention_backward(query, keys, values, weights, grad_mixed):
    factor = HEAD_DIM ** (-0.5)
    grad_weights = jnp.einsum("qhe,khe->hqk", grad_mixed, values, preferred_element_type=jnp.float32)
    grad_scores = (weights * (grad_weights - jnp.sum(weights * grad_weights, -1, keepdims=True))).astype(jnp.bfloat16)
    grad_values = jnp.einsum(
        "hqk,qhe->khe", weights.astype(jnp.bfloat16), grad_mixed, preferred_element_type=jnp.float32
    )
    grad_query = jnp.einsum("hqk,khe->qhe", grad_scores, keys, preferred_element_type=jnp.float32) * factor
    grad_keys = jnp.einsum("hqk,qhe->khe", grad_scores, query, preferred_element_type=jnp.float32) * factor
    return (grad_query, grad_keys, grad_values)


def total_rows(value):
    return jnp.sum(value.astype(jnp.float32), 0)


def plackett(scores, ranking):
    ordered = scores[ranking]
    count = ordered.shape[0]
    later = jnp.arange(count)[None, :] >= jnp.arange(count)[:, None]
    grid = jnp.where(later, ordered[None, :], MASKED)
    top_score = jnp.max(grid, 1, keepdims=True)
    tails = top_score[:, 0] + jnp.log(jnp.sum(jnp.exp(grid - top_score), 1))
    return jnp.sum(tails - ordered)


def head_pass(state, final, ranking):
    gain_vector, bias_vector, weight = (final[:D], final[D : 2 * D], final[2 * D :])
    normal, scale = standard_deviation(state)
    chosen = lax.reduce_precision(normal * gain_vector + bias_vector, 8, 7)
    scores = jnp.sum(chosen * weight, -1)
    loss, pull = jax.vjp(lambda given: plackett(given, ranking), scores)
    (grad_scores,) = pull(jnp.ones((), jnp.float32))
    grad_chosen = grad_scores[:, None] * weight
    grad_final = jnp.concatenate(
        [
            jnp.sum(grad_chosen * normal, 0),
            jnp.sum(grad_chosen, 0),
            jnp.sum(grad_scores[:, None] * chosen, 0),
        ]
    )
    return (loss, norm_gradient_pass(grad_chosen * gain_vector, normal, scale), grad_final)


def adamw_update(weight, moment, second, average, gradient_value, rate, decay):
    moment_new = BETA_ONE * moment + (1.0 - BETA_ONE) * gradient_value
    second_new = BETA_TWO * second + (1.0 - BETA_TWO) * gradient_value * gradient_value
    moment_hat = moment_new / (1.0 - BETA_ONE**STEP)
    second_hat = second_new / (1.0 - BETA_TWO**STEP)
    weight_new = weight - rate * (moment_hat / (jnp.sqrt(second_hat) + ADAM_EPS) + decay * weight)
    average_new = EMA_KEEP * average + (1.0 - EMA_KEEP) * weight_new
    return (weight_new, moment_new, second_new, average_new)


def low_rows(table, token):
    features, vocabulary = table.shape
    block = 4096

    def kernel(table_ref, token_ref, out_ref):
        out_ref[...] = table_ref[...].T.astype(jnp.bfloat16)

    return pl.pallas_call(
        kernel,
        grid=(pl.cdiv(vocabulary, block),),
        out_shape=jax.ShapeDtypeStruct((vocabulary, features), jnp.bfloat16),
        in_specs=[
            pl.BlockSpec((features, block), lambda at: (0, at)),
            pl.BlockSpec(memory_space=pl.ANY),
        ],
        out_specs=pl.BlockSpec((block, features), lambda at: (at, 0)),
        compiler_params=pltpu.CompilerParams(vmem_limit_bytes=48 * 1024 * 1024),
        name="low_rows",
    )(table, token)


def sum_rows(ids, rows, count):
    tokens, features = rows.shape
    unroll, block = 32, 384

    def kernel(ids_ref, rows_ref, out_ref, squares_ref):
        def clear(at, carry):
            out_ref[pl.ds(at * block, block), :] = jnp.zeros((block, features), jnp.float32)
            return carry

        lax.fori_loop(0, count // block, clear, 0)

        def add(at, carry):
            for step in range(unroll):
                token = at * unroll + step
                spot = ids_ref[token]
                out_ref[pl.ds(spot, 1), :] = out_ref[pl.ds(spot, 1), :] + rows_ref[pl.ds(token, 1), :]
            return carry

        lax.fori_loop(0, tokens // unroll, add, 0)

        def square(at, total):
            value = out_ref[pl.ds(at * block, block), :]
            return total + jnp.sum((value * value).reshape(block // 8, 8, features), 0)

        total = lax.fori_loop(0, count // block, square, jnp.zeros((8, features), jnp.float32))
        squares_ref[0, 0] = jnp.sum(total)

    summed, squares = pl.pallas_call(
        kernel,
        out_shape=(
            jax.ShapeDtypeStruct((count, features), jnp.float32),
            jax.ShapeDtypeStruct((1, 1), jnp.float32),
        ),
        grid_spec=pltpu.PrefetchScalarGridSpec(
            num_scalar_prefetch=1,
            grid=(1,),
            in_specs=[pl.BlockSpec((tokens, features), lambda at, ids: (0, 0))],
            out_specs=[
                pl.BlockSpec((count, features), lambda at, ids: (0, 0), pipeline_mode=pl.Buffered(1)),
                pl.BlockSpec(memory_space=pltpu.SMEM),
            ],
        ),
        compiler_params=pltpu.CompilerParams(vmem_limit_bytes=58 * 1024 * 1024),
        name="sum_rows",
    )(ids, rows)
    return (summed, squares[0, 0])


def table_update(table, moment, second, average, grad_rows, factor):
    features, vocabulary = table.shape
    block = 7296

    def kernel(factor_ref, table_ref, moment_ref, second_ref, average_ref, grad_ref, *outs):
        grad = grad_ref[...].T * factor_ref[0, 0]
        parts = adamw_update(
            table_ref[...], moment_ref[...], second_ref[...], average_ref[...], grad, RATE_MAT, WEIGHT_DECAY
        )
        for out, part in zip(outs, parts):
            out[...] = part

    wide = pl.BlockSpec((features, block), lambda at: (0, at))
    return tuple(
        pl.pallas_call(
            kernel,
            grid=(pl.cdiv(vocabulary, block),),
            out_shape=[jax.ShapeDtypeStruct(table.shape, jnp.float32)] * 4,
            in_specs=[pl.BlockSpec(memory_space=pltpu.SMEM)]
            + [wide] * 4
            + [pl.BlockSpec((block, features), lambda at: (at, 0))],
            out_specs=[wide] * 4,
            compiler_params=pltpu.CompilerParams(vmem_limit_bytes=56 * 1024 * 1024),
            name="table_update",
        )(factor.reshape(1, 1), table, moment, second, average, grad_rows)
    )


def body(
    token_ids,
    seg_lengths,
    rankings,
    table,
    table_m,
    table_v,
    table_ema,
    in_w,
    in_m,
    in_v,
    in_ema,
    out_w,
    out_m,
    out_v,
    out_ema,
    layer_vec,
    vec_m,
    vec_v,
    vec_ema,
    final_vec,
    final_m,
    final_v,
    final_ema,
):
    links = Links()
    core, place, count = links.core, links.dp, links.count
    micro, width = token_ids.shape
    mine_first = core == 0

    pace = Pace()
    low_in, low_out = in_w[0].astype(jnp.bfloat16), out_w[0].astype(jnp.bfloat16)

    def halves(shard):
        rows = shard.shape[0] // 2
        keep = lax.dynamic_slice_in_dim(shard, core * rows, rows, 0)
        give = lax.dynamic_slice_in_dim(shard, (1 - core) * rows, rows, 0)
        got = links.swap(give)
        return (jnp.where(mine_first, keep, got), jnp.where(mine_first, got, keep))

    in_0, in_1 = halves(low_in)
    out_0, out_1 = halves(low_out)
    own_vec, own_final = lax.reduce_precision(layer_vec[0], 8, 7), lax.reduce_precision(final_vec, 8, 7)
    vec_part, final_part = own_vec.shape[0], own_final.shape[0]
    small = Small(links, jnp.concatenate([own_vec, own_final, token_ids.astype(jnp.float32).reshape(-1)]))
    pace.close(in_0, out_0, *small.along(pace))
    w_in_0 = lax.all_gather(in_0, ("dp", "section"), axis=0, tiled=True)
    w_up_1 = lax.all_gather(in_1[:, 3 * D :], ("dp", "section"), axis=0, tiled=True)
    w_out_1 = lax.all_gather(out_1, ("dp", "section"), axis=0, tiled=True)
    out_0, qkv_1 = Gather(links, out_0), Gather(links, in_1[:, : 3 * D])
    pace.close(*small.along(pace))
    table_rows = low_rows(table, pace.token)
    pace.close(*small.along(pace), peek(table_rows))
    pace.close(*small.wave(pace))
    pace.close(*small.wave(pace))
    lengths = lax.dynamic_slice_in_dim(seg_lengths, core, 1, 0)[0]
    small = small.whole(pace)
    small_other = links.swap(small[:, :vec_part])
    own_layer, other_layer = small[:, :vec_part].reshape(-1), small_other.reshape(-1)
    vector_0 = jnp.where(mine_first, own_layer, other_layer)
    vector_1 = jnp.where(mine_first, other_layer, own_layer)
    final = small[:, vec_part : vec_part + final_part].reshape(-1)
    every_ids = small[:, vec_part + final_part :].astype(jnp.int32).reshape(count, micro, width)

    ids_here = lax.dynamic_slice_in_dim(every_ids, core, 1, 1).reshape(-1)
    picked = jnp.take(table_rows, pace.tie(ids_here), axis=0, mode="clip")
    features = picked.shape[1]
    blocks = picked.reshape(links.sizes + (width, features)).transpose(0, 1, 2, 4, 3)
    pace.close(peek(blocks), *out_0.along(pace, 1))
    blocks = exchange_along(links, pace.tie(blocks), 2)
    pace.close(peek(blocks), *out_0.along(pace, 1))
    blocks = exchange_along(links, pace.tie(blocks), 1)
    pace.close(peek(blocks), *out_0.along(pace))
    blocks = exchange_along(links, pace.tie(blocks), 0)
    pace.close(peek(blocks))
    state = blocks.reshape(D, width).T.astype(jnp.float32)

    ranking = lax.dynamic_slice_in_dim(rankings, core, 1, 0)[0]
    position, allowed, last = layout(lengths, width)
    cosine, sine = angles(position)

    first_gain, first_bias, second_gain, second_bias, bias_qkv, bias_attn, bias_up, bias_down = pieces(vector_0)
    normal, scale = standard_deviation(state)
    left = (normal * first_gain + first_bias).astype(jnp.bfloat16)
    right = (normal * second_gain + second_bias).astype(jnp.bfloat16)
    joined = matmul(pace.tie(left), w_in_0[:, : 3 * D]) + bias_qkv
    tables, seen = spin_tables(cosine, sine), allowed.astype(jnp.float32)
    query, keys, values, mixed = attend(joined, tables, seen)
    pace.close(*out_0.wave(pace), *qkv_1.along(pace, 1), peek(mixed))
    upper = matmul(pace.tie(right), w_in_0[:, 3 * D :]) + bias_up
    active = jax.nn.gelu(upper, approximate=False).astype(jnp.bfloat16)
    pace.close(*out_0.wave(pace), *qkv_1.along(pace, 1), peek(active))
    left_both = both_rows(links, relative_rows(links, left))
    right_both = both_rows(links, relative_rows(links, right))
    pace.close(*out_0.last(pace), *qkv_1.along(pace), peek(left_both), peek(right_both))
    w_out_0 = out_0.whole()
    acts = jnp.concatenate([mixed, active], 1)
    state_1 = (
        state + matmul(mixed, w_out_0[:D]) + bias_attn + (matmul(pace.tie(active), w_out_0[D:]) + bias_down)
    )
    state_1 = lax.reduce_precision(state_1, 8, 7)
    kept = (normal, scale, left, right, upper, query, keys, values, acts)
    pace.close(*qkv_1.wave(pace), peek(state_1))
    pace.close(*qkv_1.wave(pace))
    pace.close(*qkv_1.last(pace))
    w_qkv_1 = qkv_1.whole()
    state_1 = pace.tie(state_1)

    ends = last.shape[0]
    first_gain, first_bias, second_gain, second_bias, bias_qkv, bias_attn, bias_up, bias_down = pieces(vector_1)
    normal, scale = standard_deviation(state_1)
    left = (normal * first_gain + first_bias).astype(jnp.bfloat16)
    pairs = matmul(left, w_qkv_1[:, D:]) + bias_qkv[D:]
    keys = turn(pairs[:, :D].reshape(width, HEADS, HEAD_DIM), cosine, sine, 1.0).astype(jnp.bfloat16)
    values = pairs[:, D:].reshape(width, HEADS, HEAD_DIM).astype(jnp.bfloat16)
    normal_end, scale_end, state_end = normal[last], scale[last], state_1[last]
    cosine_end, sine_end, allowed_end = cosine[last], sine[last], allowed[last]
    left_end = (normal_end * first_gain + first_bias).astype(jnp.bfloat16)
    right_end = (normal_end * second_gain + second_bias).astype(jnp.bfloat16)
    query = matmul(left_end, w_qkv_1[:, :D]) + bias_qkv[:D]
    query = turn(query.reshape(ends, HEADS, HEAD_DIM), cosine_end, sine_end, 1.0).astype(jnp.bfloat16)
    upper = matmul(right_end, w_up_1) + bias_up
    weights = softmax_parts(scores_of(query, keys, allowed_end))
    mixed = (
        jnp.einsum("hqk,khe->qhe", weights.astype(jnp.bfloat16), values, preferred_element_type=jnp.float32)
        .reshape(ends, D)
        .astype(jnp.bfloat16)
    )
    active = jax.nn.gelu(upper, approximate=False).astype(jnp.bfloat16)
    branch = matmul(mixed, w_out_1[:D]) + bias_attn + (matmul(active, w_out_1[D:]) + bias_down)
    loss, grad_end, grad_final = head_pass(state_end + branch, final, ranking)

    low_end = grad_end.astype(jnp.bfloat16)
    grad_mixed = dot_cols(low_end, w_out_1[:D]).astype(jnp.bfloat16).reshape(ends, HEADS, HEAD_DIM)
    grad_upper = (dot_cols(low_end, w_out_1[D:]) * gelu_slope(upper)).astype(jnp.bfloat16)
    grad_query, grad_keys, grad_values = attention_backward(query, keys, values, weights, grad_mixed)
    grad_query = turn(grad_query, cosine_end, sine_end, -1.0).reshape(ends, D).astype(jnp.bfloat16)
    grad_pairs = jnp.concatenate(
        [turn(grad_keys, cosine, sine, -1.0).reshape(width, D), grad_values.reshape(width, D)], 1
    ).astype(jnp.bfloat16)
    back_left = dot_cols(grad_pairs, w_qkv_1[:, D:])
    back_left_end = dot_cols(grad_query, w_qkv_1[:, :D])
    back_right_end = dot_cols(grad_upper, w_up_1)
    sum_end = total_rows(low_end)
    sum_vec_1 = jnp.concatenate(
        [
            jnp.sum(back_left * normal, 0) + jnp.sum(back_left_end * normal_end, 0),
            jnp.sum(back_left, 0) + jnp.sum(back_left_end, 0),
            jnp.sum(back_right_end * normal_end, 0),
            jnp.sum(back_right_end, 0),
            total_rows(grad_query),
            total_rows(grad_pairs),
            sum_end,
            total_rows(grad_upper),
            sum_end,
        ]
    )
    row_index = jnp.arange(width, dtype=jnp.int32)
    extra = back_left_end * first_gain + back_right_end * second_gain
    pulled = back_left * first_gain
    landed = jnp.zeros_like(pulled)
    for end in range(ends):
        here = (row_index == last[end])[:, None]
        pulled = pulled + jnp.where(here, extra[end][None], 0.0)
        landed = landed + jnp.where(here, grad_end[end][None], 0.0)
    grad_state = landed + norm_gradient_pass(pulled, normal, scale)
    grad_state = lax.reduce_precision(grad_state, 8, 7).astype(jnp.bfloat16)

    pairs_both = both_rows(links, relative_rows(links, left))
    pairs_grad = jnp.concatenate([grad_pairs, links.swap(grad_pairs)])
    factors = jnp.concatenate([left_end, right_end, mixed, active, grad_query, grad_upper, low_end], 1)
    every_factor = lax.all_gather(factors, ("dp", "section"), axis=0, tiled=True)
    in_rows, out_rows = in_w.shape[1], out_w.shape[1]

    normal, scale, left, right, upper, query, keys, values, acts = kept
    first_gain, first_bias, second_gain, second_bias = pieces(vector_0)[:4]
    low_state = grad_state
    pair_sum = Reduce(links, halves_total(pairs_both, pairs_grad), "baz")
    pace.close(peek(pair_sum.moving), peek(low_state))
    low_state = pace.tie(low_state)
    out_half = dot_rows(acts, low_state).astype(jnp.bfloat16)
    out_half = lax.psum_scatter(out_half, ("dp", "section"), scatter_dimension=0, tiled=True)
    grad_mixed = dot_cols(low_state, w_out_0[:D]).astype(jnp.bfloat16)
    grad_upper = (dot_cols(low_state, w_out_0[D:]) * gelu_slope(upper)).astype(jnp.bfloat16)
    upper_both = jnp.concatenate([grad_upper, links.swap(grad_upper)])
    pace.close(*map(peek, pair_sum.ring(pace)), peek(grad_mixed), peek(upper_both))
    up_sum = halves_total(right_both, pace.tie(upper_both))
    grad_joined = attend_back(query, keys, values, pace.tie(grad_mixed), tables, seen)
    pace.close(*map(peek, pair_sum.ring(pace)), peek(up_sum), peek(grad_joined))
    grad_joined = pace.tie(grad_joined)
    back_left = dot_cols(grad_joined, w_in_0[:, : 3 * D])
    back_right = dot_cols(grad_upper, w_in_0[:, 3 * D :])
    grad_embedded = low_state.astype(jnp.float32) + norm_gradient_pass(
        back_left * first_gain + back_right * second_gain, normal, scale
    )
    joined_both = jnp.concatenate([grad_joined, links.swap(grad_joined)])
    blocks = grad_embedded.astype(jnp.bfloat16).T.reshape(links.sizes + (features, width))
    pace.close(*map(peek, pair_sum.step(pace)), peek(joined_both), peek(blocks))
    blocks = exchange_along(links, pace.tie(blocks), 2)
    qkv_sum = halves_total(left_both, pace.tie(joined_both))
    pace.close(*map(peek, pair_sum.step(pace)), peek(blocks), peek(qkv_sum))
    rest_sum = Reduce(links, jnp.concatenate([qkv_sum, up_sum], 4), "baz")
    blocks = exchange_along(links, pace.tie(blocks), 1)
    back_left, back_right = pace.tie(back_left), pace.tie(back_right)
    sum_state = total_rows(low_state)
    sum_vec_0 = jnp.concatenate(
        [
            jnp.sum(back_left * normal, 0),
            jnp.sum(back_left, 0),
            jnp.sum(back_right * normal, 0),
            jnp.sum(back_right, 0),
            total_rows(grad_joined),
            sum_state,
            total_rows(grad_upper),
            sum_state,
        ]
    )
    packed = jnp.concatenate([sum_vec_0, sum_vec_1, grad_final, loss[None], jnp.zeros((127,), jnp.float32)])
    packed = Total(links, packed.reshape(-1, 128))
    pace.close(*map(peek, pair_sum.step(pace)), peek(blocks), packed.value)
    blocks = exchange_along(links, pace.tie(blocks), 0)
    first = rest_sum.ring(pace)
    pace.close(peek(blocks), *packed.step(pace))
    blocks = pace.tie(blocks)
    spread_mine = blocks.reshape(count, features, width).transpose(0, 2, 1)
    spread_other = links.swap(spread_mine)
    spread = jnp.stack(
        [jnp.where(mine_first, spread_mine, spread_other), jnp.where(mine_first, spread_other, spread_mine)], 1
    ).reshape(count * micro * width, features)
    table_grad, table_squares = sum_rows(every_ids.reshape(-1), spread.astype(jnp.float32), table.shape[1])
    pace.close(*map(peek, first), peek(table_grad), *packed.step(pace))
    pace.close(*map(peek, rest_sum.ring(pace)), *packed.step(pace))
    pace.close(*map(peek, rest_sum.step(pace)), *packed.step(pace))
    pace.close(*map(peek, rest_sum.step(pace)), *packed.step(pace))
    pace.close(*map(peek, rest_sum.ring(pace)), *packed.step(pace))
    in_half, pair_half = rest_sum.done(pace), pair_sum.done(pace)

    def factor_part(begin, size):
        return every_factor[:, begin : begin + size]

    left_own = lax.dynamic_slice_in_dim(factor_part(0, D), place * in_rows, in_rows, 1)
    right_own = lax.dynamic_slice_in_dim(factor_part(D, D), place * in_rows, in_rows, 1)
    acts_own = lax.dynamic_slice_in_dim(factor_part(2 * D, D + FF), place * out_rows, out_rows, 1)
    query_part = factor_part(3 * D + FF, D)
    upper_part = factor_part(4 * D + FF, FF)
    end_part = factor_part(4 * D + 2 * FF, D)
    grad_in_query = dot_rows(left_own, query_part)
    grad_in_upper = dot_rows(right_own, upper_part)
    grad_out_1 = dot_rows(acts_own, end_part)


    packed = packed.done(pace).reshape(-1)
    vec_size = sum_vec_0.shape[0]
    shard_vec = lax.dynamic_slice_in_dim(packed, core * vec_size + place * vec_part, vec_part, 0)
    shard_fin = lax.dynamic_slice_in_dim(packed, 2 * vec_size + place * final_part, final_part, 0)
    loss_sum = packed[2 * vec_size + 3 * D]

    in_other, out_other, pair_other = links.swap(in_half), links.swap(out_half), links.swap(pair_half)
    grad_in_0 = jnp.concatenate([in_half, in_other], 0)
    out_half = out_half.astype(jnp.float32)
    grad_out_0 = jnp.concatenate([out_half, out_other.astype(jnp.float32)], 0)
    grad_in_1 = jnp.concatenate(
        [grad_in_query, jnp.concatenate([pair_other, pair_half], 0), grad_in_upper], 1
    )
    shard_in = jnp.where(mine_first, grad_in_0, grad_in_1)
    shard_out = jnp.where(mine_first, grad_out_0, grad_out_1)

    squares = (
        jnp.sum(shard_in * shard_in)
        + jnp.sum(shard_out * shard_out)
        + jnp.sum(shard_vec * shard_vec)
        + jnp.where(mine_first, table_squares + jnp.sum(shard_fin * shard_fin), 0.0)
    )
    total_squares = all_sum(links, jnp.broadcast_to(squares, (8, 128)))[0, 0]
    grad_norm = jnp.sqrt(total_squares)
    factor = jnp.minimum(1.0, CLIP_NORM / (grad_norm + 1e-06))
    table_parts = table_update(table, table_m, table_v, table_ema, table_grad, factor)
    in_parts = adamw_update(
        in_w, in_m, in_v, in_ema, shard_in.reshape(in_w.shape) * factor, RATE_MAT, WEIGHT_DECAY
    )
    out_parts = adamw_update(
        out_w, out_m, out_v, out_ema, shard_out.reshape(out_w.shape) * factor, RATE_MAT, WEIGHT_DECAY
    )
    vec_parts = adamw_update(
        layer_vec, vec_m, vec_v, vec_ema, shard_vec.reshape(layer_vec.shape) * factor, RATE_VEC, 0.0
    )
    final_parts = adamw_update(final_vec, final_m, final_v, final_ema, shard_fin * factor, RATE_VEC, 0.0)
    return (loss_sum, grad_norm) + table_parts + in_parts + out_parts + vec_parts + final_parts


def solution(mesh):
    in_specs = (
        P("dp", None),
        P("dp", None),
        P("dp", None),
        P("dp", None),
        P("dp", None),
        P("dp", None),
        P("dp", None),
        P("section", "dp", None),
        P("section", "dp", None),
        P("section", "dp", None),
        P("section", "dp", None),
        P("section", "dp", None),
        P("section", "dp", None),
        P("section", "dp", None),
        P("section", "dp", None),
        P("section", "dp"),
        P("section", "dp"),
        P("section", "dp"),
        P("section", "dp"),
        P("dp"),
        P("dp"),
        P("dp"),
        P("dp"),
    )
    out_specs = (
        P(),
        P(),
        P("dp", None),
        P("dp", None),
        P("dp", None),
        P("dp", None),
        P("section", "dp", None),
        P("section", "dp", None),
        P("section", "dp", None),
        P("section", "dp", None),
        P("section", "dp", None),
        P("section", "dp", None),
        P("section", "dp", None),
        P("section", "dp", None),
        P("section", "dp"),
        P("section", "dp"),
        P("section", "dp"),
        P("section", "dp"),
        P("dp"),
        P("dp"),
        P("dp"),
        P("dp"),
    )
    return jax.shard_map(body, mesh=mesh, in_specs=in_specs, out_specs=out_specs, check_vma=False)
```
